128 devices in a mesh: row: 8 (over y_lo, x), col: 16 (over z, y_hi, core).
Axes of the slice: x: 4, y: 4 (y_hi: 2, y_lo: 2; y = y_hi * 2 + y_lo), z: 4, core: 2. Of those that a mesh axis runs over, the one named last changes fastest.
Arguments:
- pair_products: bfloat16 [2, 46080, 512], P(None, 'row', 'col'), may hold values from -6 to 6
- eigvecs: bfloat16 [46080, 4608], P('row', 'col'), may hold values from -0.02734375 to 0.02734375
- valence_band: int32 [2, 64], replicated, may hold values from 0 to 5483
- cond_band: int32 [2, 8], replicated, may hold values from 0 to 4095
- valence_energy: float32 [5484], replicated, may hold values from -15 to -0.5
- cond_energy: float32 [4096], replicated, may hold values from 0.5 to 20
Outputs:
- chi: float32 [12, 4608, 4608], P(None, 'row', 'col')
The draws below stay inside these ranges and needn't reach their ends.
All inputs are finite; a program needn't handle non-finite values.
Results may differ from the reference program's by a relative error of at most 0.0045.
Values may be sent and summed in bfloat16 or wider, within the bound.
A program may use at most 64 MiB of HBM per device.

```python
import jax
import jax.numpy as jnp

NG = 46080
NS = 4608
NV = 64
NC = 8
NFREQ = 12
NBLK = 2
NVAL = 5484
NCON = 4096
NPAIR = 512


def with_ends(values, key, least, largest):
    spot = [jax.random.randint(jax.random.fold_in(key, axis), (), 0, length) for axis, length in enumerate(values.shape)]
    main_axis = values.shape.index(max(values.shape))
    beside = spot[:main_axis] + [(spot[main_axis] + 1) % values.shape[main_axis]] + spot[main_axis + 1:]
    return values.at[tuple(spot)].set(least).at[tuple(beside)].set(largest)


def block_levels(rng, shape, shards, low, high):
    level = 1.0
    for dim, blocks in shards:
        draws = jax.random.uniform(jax.random.fold_in(jax.random.fold_in(rng, 6), dim), (blocks,), jnp.float32, low / len(shards), high / len(shards))
        level = level * jnp.repeat(jnp.exp(draws), shape[dim] // blocks).reshape((-1,) + (1,) * (len(shape) - 1 - dim))
    return level


def bell_draw(own_key, shape, width, limit, shards=(), dtype=jnp.bfloat16):
    factor_of = block_levels(own_key, shape, shards, -0.22, 0.18) if shards else 1.0
    result = jax.random.normal(own_key, shape, jnp.float32) * width * factor_of
    return jnp.minimum(jnp.maximum(result, -limit), limit).astype(dtype)


def setup_inputs(seed: int = 0) -> dict:
    streams_of = jax.random.split(jax.random.key(seed), 7)
    pair_products = bell_draw(streams_of[0], (NBLK, NG, NPAIR), 1.0, 6.0, ((1, 8), (2, 16)))
    eigvecs = bell_draw(streams_of[1], (NG, NS), NG ** -0.5, 0.02734375, ((0, 8), (1, 16)))
    valence_band = with_ends(jax.random.randint(streams_of[2], (NBLK, NV), 0, NVAL), jax.random.fold_in(streams_of[2], 1), 0, NVAL - 1).astype(jnp.int32)
    cond_band = with_ends(jax.random.randint(streams_of[3], (NBLK, NC), 0, NCON), jax.random.fold_in(streams_of[3], 1), 0, NCON - 1).astype(jnp.int32)
    valence_energy = jnp.clip(jax.random.uniform(streams_of[4], (NVAL,), jnp.float32, -15.0, -0.5), -15.0, -0.5)
    cond_energy = jnp.clip(jax.random.uniform(streams_of[5], (NCON,), jnp.float32, 0.5, 20.0), 0.5, 20.0)
    return dict(pair_products=pair_products, eigvecs=eigvecs, valence_band=valence_band, cond_band=cond_band, valence_energy=valence_energy, cond_energy=cond_energy)


def pair_factor(valence_band, cond_band, valence_energy, cond_energy):
    low = jnp.take(valence_energy, valence_band, axis=0)
    high = jnp.take(cond_energy, cond_band, axis=0)
    delta = (high[:, None, :] - low[:, :, None]).reshape(NBLK, NV * NC)
    omega = 1.5 * jnp.arange(NFREQ).astype(jnp.float32)
    scale = 1.0 / jnp.sqrt(jnp.float32(NBLK * NV * NC))
    return -4.0 * delta[:, None, :] / (delta[:, None, :] ** 2 + omega[None, :, None] ** 2) * scale

def reference(pair_products, eigvecs, valence_band, cond_band, valence_energy, cond_energy):
    factor = pair_factor(valence_band, cond_band, valence_energy, cond_energy)
    totals = [jnp.zeros((NS, NS), jnp.float32) for w in range(NFREQ)]
    for blk in range(NBLK):
        projected = jnp.dot(eigvecs.T, pair_products[blk], preferred_element_type=jnp.float32).astype(jnp.bfloat16)
        wide = projected.astype(jnp.float32)
        for w in range(NFREQ):
            scaled = (wide * factor[blk, w][None, :]).astype(jnp.bfloat16)
            totals[w] = totals[w] + jnp.dot(scaled, projected.T, preferred_element_type=jnp.float32)
    return jnp.stack(totals, axis=0)
```

```python
import jax
import jax.numpy as jnp
from jax import lax
from jax.experimental import pallas as pl
from jax.experimental.pallas import tpu as pltpu
from jax.sharding import PartitionSpec as P

NFREQ = 12
MESH = pl.DeviceIdType.MESH
LANE = 128
TA1, TA2, TB1, TB2 = 13, 13, 10, 9
SLICE = 16


def pair_factor(valence_band, cond_band, valence_energy, cond_energy):
    nblk = valence_band.shape[0]
    nval = valence_energy.shape[0]
    ncon = cond_energy.shape[0]
    val_hot = valence_band[:, :, None] == jnp.arange(nval, dtype=jnp.int32)[None, None, :]
    con_hot = cond_band[:, :, None] == jnp.arange(ncon, dtype=jnp.int32)[None, None, :]
    low = jnp.sum(jnp.where(val_hot, valence_energy[None, None, :], 0.0), axis=2)
    high = jnp.sum(jnp.where(con_hot, cond_energy[None, None, :], 0.0), axis=2)
    low = low.reshape(nblk, 8, 2, 4).transpose(2, 1, 0, 3)
    delta = (high[None, None, :, None, :] - low[:, :, :, :, None]).reshape(1, -1)
    omega = 1.5 * jnp.arange(NFREQ).astype(jnp.float32)
    scale = 1.0 / jnp.sqrt(jnp.float32(delta.shape[1]))
    return -4.0 * delta / (delta**2 + omega[:, None] ** 2) * scale


def project_kernel(p_hbm, e_hbm, rows_out, cols_out, pairs, eig, total, landed, halves, spread,
                   gather_send, gather_recv, copy_sem, eig_send, eig_recv, sum_send, sum_recv,
                   spread_send, spread_recv, cols_send, cols_recv, rows_send, rows_recv, local_sem):
    row, col = lax.axis_index("row"), lax.axis_index("col")
    core = lax.rem(col, 2)
    j = col // 2
    z, h = j // 2, lax.rem(j, 2)
    ylo = row // 4
    m_half = e_hbm.shape[0]
    m_all = 2 * m_half

    def seat(zz, hh, cc):
        return (row, zz * 4 + hh * 2 + cc)

    up = seat(lax.rem(z + 1, 4), h, core)
    down = seat(lax.rem(z + 3, 4), h, core)
    across = seat(z, 1 - h, core)
    twin = (row, col + 1 - 2 * core)

    block_rows = p_hbm.shape[1]
    local = [
        pltpu.make_async_copy(p_hbm.at[b], pairs.at[pl.ds(b * block_rows, block_rows)], copy_sem.at[b])
        for b in range(2)
    ]
    mine = pl.ds(pl.multiple_of(core * m_half, 16), m_half)
    local.append(pltpu.make_async_copy(e_hbm, eig.at[mine], copy_sem.at[2]))
    for c in local:
        c.start()

    barrier = pltpu.get_barrier_semaphore()

    def greet_rows(d, carry):
        other = lax.rem(row + d, 8)
        for c in range(2):
            pl.semaphore_signal(barrier, inc=1, device_id=(other, j * 2 + c), device_id_type=MESH)
        return carry

    def greet_cols(d, carry):
        other = lax.rem(j + d, 8)
        pl.semaphore_signal(barrier, inc=1, device_id=(row, other * 2 + core), device_id_type=MESH)
        return carry

    lax.fori_loop(1, 8, greet_rows, 0)
    lax.fori_loop(1, 8, greet_cols, 0)
    pl.semaphore_signal(barrier, inc=1, device_id=twin, device_id_type=MESH)
    pl.semaphore_wait(barrier, 22)

    eig_copy = pltpu.make_async_remote_copy(
        e_hbm, eig.at[mine], eig_send, eig_recv, device_id=twin, device_id_type=MESH
    )

    a0, a1, a2 = 0, TA1 * LANE, (TA1 + TA2) * LANE
    b1, b2 = a2 + TB1 * LANE, a2 + (TB1 + TB2) * LANE
    piece = {"A": (a0, a2), "A1": (a0, a1), "A2": (a1, a2), "B": (a2, b2), "B1": (a2, b1), "B2": (b1, b2)}

    slot_of = {(0, 0): 0, (0, 1): 1, (1, 0): 2, (3, 0): 3, (1, 1): 4, (3, 1): 5, (2, 0): 6, (2, 1): 7}
    place_of = {s: k for k, s in slot_of.items()}
    copies = {}

    def region(slot, name):
        lo, hi = piece[name]
        return pairs.at[pl.ds(64 * slot, 64), pl.ds(lo, hi - lo)]

    def send(slot, name, way):
        dz, dh = place_of[slot]
        target, there = {
            "up": (up, ((dz + 3) % 4, dh)),
            "down": (down, ((dz + 1) % 4, dh)),
            "across": (across, (dz, 1 - dh)),
        }[way]
        there = slot_of[there]
        n = len(copies)
        c = pltpu.make_async_remote_copy(
            region(slot, name), region(there, name), gather_send.at[n], gather_recv.at[n],
            device_id=target, device_id_type=MESH,
        )
        copies[(there, name)] = c
        c.start()

    def arrive(slot, name):
        copies[(slot, name)].wait_recv()

    def multiply(g, name):
        lo, hi = piece[name]
        rows = pl.ds(128 * g, 128)
        value = lax.dot_general(
            pairs[rows, lo:hi], eig[:, lo:hi], (((1,), (1,)), ((), ())), preferred_element_type=jnp.float32
        )
        if name == "B":
            total[rows, :] = value
        else:
            total[rows, :] += value

    def pair_row(g, owner, jj, cc):
        yo = owner // 4
        if g == 0:
            dz, dh = 0, yo
        elif g == 3:
            dz, dh = 2, yo
        else:
            dz, dh = 1 + 2 * yo, g - 1
        zz = lax.rem(jj // 2 + dz, 4)
        hh = lax.rem(lax.rem(jj, 2) + dh, 2)
        return pl.multiple_of(cc * 512 + (zz * 2 + hh) * 64 + lax.rem(owner, 4) * SLICE, SLICE)

    def sum_start(g):
        def go(d, carry):
            to = lax.rem(row + d, 8)
            pltpu.make_async_remote_copy(
                total.at[pl.ds(pl.multiple_of(128 * g + to * SLICE, SLICE), SLICE)],
                landed.at[g, pl.ds(pl.multiple_of((d - 1) * SLICE, SLICE), SLICE)],
                sum_send.at[g], sum_recv.at[g],
                device_id=(to, col), device_id_type=MESH,
            ).start()
            return carry

        lax.fori_loop(1, 8, go, 0)

    def sum_end(g):
        seven = landed.at[g]
        pltpu.make_async_copy(seven, seven, sum_recv.at[g]).wait()
        value = total[pl.ds(pl.multiple_of(128 * g + row * SLICE, SLICE), SLICE), :]
        for d in range(7):
            value = value + landed[g, d * SLICE:(d + 1) * SLICE, :]
        value = value.astype(spread.dtype)
        spread[g, 0] = value
        halves[g, 0] = value[:, :m_half]
        halves[g, 1] = value[:, m_half:]

        def go(d, carry):
            to = lax.rem(j + d, 8)
            pltpu.make_async_remote_copy(
                spread.at[g, 0], spread.at[g, d], spread_send.at[g], spread_recv.at[g],
                device_id=(row, to * 2 + core), device_id_type=MESH,
            ).start()
            return carry

        lax.fori_loop(1, 8, go, 0)
        first = pair_row(g, row, j, core)

        def go_cols(d, carry):
            to = lax.rem(row + d, 8)
            for c in range(2):
                pltpu.make_async_remote_copy(
                    halves.at[g, c], cols_out.at[pl.ds(first, SLICE)], cols_send, cols_recv,
                    device_id=(to, j * 2 + c), device_id_type=MESH,
                ).start()
            return carry

        lax.fori_loop(1, 8, go_cols, 0)
        pltpu.make_async_remote_copy(
            halves.at[g, 1 - core], cols_out.at[pl.ds(first, SLICE)], cols_send, cols_recv,
            device_id=twin, device_id_type=MESH,
        ).start()
        pltpu.make_async_copy(halves.at[g, core], cols_out.at[pl.ds(first, SLICE)], local_sem.at[g]).start()

    def deal(g):
        seven = spread.at[g, pl.ds(1, 7)]
        pltpu.make_async_copy(seven, seven, spread_recv.at[g]).wait()

        def go(d, carry):
            to = lax.rem(row + d, 8)
            first = pair_row(g, row, to, core)
            for c in range(2):
                pltpu.make_async_remote_copy(
                    spread.at[g, lax.rem(j + 8 - to, 8)], rows_out.at[pl.ds(first, SLICE)], rows_send, rows_recv,
                    device_id=(to, j * 2 + c), device_id_type=MESH,
                ).start()
            return carry

        lax.fori_loop(1, 8, go, 0)
        first = pair_row(g, row, row, core)
        kept = spread.at[g, lax.rem(j + 8 - row, 8)]
        pltpu.make_async_remote_copy(
            kept, rows_out.at[pl.ds(first, SLICE)], rows_send, rows_recv, device_id=twin, device_id_type=MESH
        ).start()
        pltpu.make_async_copy(kept, rows_out.at[pl.ds(first, SLICE)], local_sem.at[4 + g]).start()

    local[0].wait()
    local[1].wait()
    send(0, "B", "up")
    send(0, "B", "down")
    send(0, "A", "across")
    eig_copy.start()
    arrive(3, "B")
    send(0, "A", "up")
    send(3, "B1", "up")
    arrive(2, "B")
    send(0, "A", "down")
    send(2, "B2", "down")
    send(0, "B", "across")
    arrive(1, "A")
    send(3, "B", "across")
    local[2].wait()
    eig_copy.wait()
    arrive(1, "B")
    send(2, "B", "across")
    multiply(0, "B")
    arrive(6, "B1")
    arrive(6, "B2")
    send(6, "B1", "across")
    send(6, "B2", "across")
    multiply(0, "A1")
    arrive(3, "A")
    send(1, "A", "up")
    send(3, "A1", "up")
    arrive(2, "A")
    send(1, "A", "down")
    send(2, "A2", "down")
    multiply(0, "A2")
    sum_start(0)
    multiply(1, "B")
    multiply(1, "A1")
    multiply(1, "A2")
    sum_start(1)
    sum_end(0)
    arrive(5, "B")
    arrive(4, "B")
    multiply(2, "B")
    sum_end(1)
    deal(0)
    arrive(5, "A")
    send(5, "A1", "up")
    arrive(4, "A")
    send(4, "A2", "down")
    multiply(2, "A1")
    multiply(2, "A2")
    sum_start(2)
    deal(1)
    arrive(7, "B1")
    arrive(7, "B2")
    multiply(3, "B")
    sum_end(2)
    arrive(6, "A1")
    arrive(7, "A1")
    multiply(3, "A1")
    arrive(6, "A2")
    arrive(7, "A2")
    multiply(3, "A2")
    sum_start(3)
    deal(2)
    sum_end(3)
    deal(3)

    for c in copies.values():
        c.wait_send()
    for g in range(4):
        seven = landed.at[g]
        pltpu.make_async_copy(seven, seven, sum_send.at[g]).wait()
        seven = spread.at[g, pl.ds(1, 7)]
        pltpu.make_async_copy(seven, seven, spread_send.at[g]).wait()
        pltpu.make_async_copy(halves.at[g, 0], cols_out.at[pl.ds(0, SLICE)], local_sem.at[g]).wait()
        pltpu.make_async_copy(spread.at[g, 0], rows_out.at[pl.ds(0, SLICE)], local_sem.at[4 + g]).wait()
    many = pl.ds(0, 60 * SLICE)
    for ref, s in ((cols_out, cols_send), (cols_out, cols_recv), (rows_out, rows_send), (rows_out, rows_recv)):
        pltpu.make_async_copy(ref.at[many], ref.at[many], s).wait()


def project(pairs_t, eig_t):
    nblk, pair_rows, depth = pairs_t.shape
    m_half = eig_t.shape[0]
    m_all = 2 * m_half
    bf16, f32 = jnp.bfloat16, jnp.float32
    dma = pltpu.SemaphoreType.DMA
    return pl.pallas_call(
        project_kernel,
        out_shape=(
            jax.ShapeDtypeStruct((1024, m_all), bf16),
            jax.ShapeDtypeStruct((1024, m_half), bf16),
        ),
        in_specs=[pl.BlockSpec(memory_space=pl.ANY)] * 2,
        out_specs=(pl.BlockSpec(memory_space=pl.ANY),) * 2,
        scratch_shapes=[
            pltpu.VMEM((512, depth), bf16),
            pltpu.VMEM((m_all, depth), bf16),
            pltpu.VMEM((512, m_all), f32),
            pltpu.VMEM((4, 7 * SLICE, m_all), f32),
            pltpu.VMEM((4, 2, SLICE, m_half), bf16),
            pltpu.VMEM((4, 8, SLICE, m_all), bf16),
            dma((18,)), dma((18,)), dma((3,)), dma, dma, dma((4,)), dma((4,)),
            dma((4,)), dma((4,)), dma, dma, dma, dma, dma((8,)),
        ],
        compiler_params=pltpu.CompilerParams(
            collective_id=0, has_side_effects=True, vmem_limit_bytes=48 * 2**20
        ),
        name="project",
    )(pairs_t, eig_t)


def chi_kernel(factor_ref, rows_ref, cols_ref, out_ref, cols_t):
    @pl.when(pl.program_id(0) == 0)
    def _():
        cols_t[...] = cols_ref[...].astype(jnp.float32).T

    scaled = (cols_t[...] * factor_ref[pl.ds(pl.program_id(0), 1), :]).astype(jnp.bfloat16)
    out_ref[0] = jnp.dot(scaled, rows_ref[...], preferred_element_type=jnp.float32)


def polarizability(factor, rows, cols):
    n, s_rows = rows.shape
    s_cols = cols.shape[1]
    return pl.pallas_call(
        chi_kernel,
        grid=(NFREQ,),
        out_shape=jax.ShapeDtypeStruct((NFREQ, s_cols, s_rows), jnp.float32),
        in_specs=[
            pl.BlockSpec((NFREQ, n), lambda w: (0, 0)),
            pl.BlockSpec((n, s_rows), lambda w: (0, 0)),
            pl.BlockSpec((n, s_cols), lambda w: (0, 0)),
        ],
        out_specs=pl.BlockSpec((1, s_cols, s_rows), lambda w: (w, 0, 0)),
        scratch_shapes=[pltpu.VMEM((s_cols, n), jnp.float32)],
        compiler_params=pltpu.CompilerParams(vmem_limit_bytes=32 * 2**20),
        name="chi",
    )(factor, rows, cols)


def local(pair_products, eigvecs, valence_band, cond_band, valence_energy, cond_energy):
    factor = pair_factor(valence_band, cond_band, valence_energy, cond_energy)
    rows, cols = project(pair_products.transpose(0, 2, 1), eigvecs.T)
    return polarizability(factor, rows, cols).transpose(0, 2, 1)


def solution(mesh):
    return jax.shard_map(
        local,
        mesh=mesh,
        in_specs=(P(None, "row", "col"), P("row", "col"), P(), P(), P(), P()),
        out_specs=P(None, "row", "col"),
        check_vma=False,
    )
```

```python
import functools

import jax
import jax.numpy as jnp
from jax import lax
from jax.experimental import pallas as pl
from jax.experimental.pallas import tpu as pltpu
from jax.sharding import PartitionSpec as P

NFREQ = 12
STEP = 3
MESH = pl.DeviceIdType.MESH
LANE = 128
TA1, TA2, TB1, TB2 = 14, 14, 9, 8
GROUP = (0, 64, 128, 256, 384, 448)
QUARTER = (16, 16, 32, 32, 16, 16)
NG = len(GROUP)
BOTH = (5,)


def pair_factor(valence_band, cond_band, valence_energy, cond_energy):
    nblk = valence_band.shape[0]
    nval = valence_energy.shape[0]
    ncon = cond_energy.shape[0]
    val_hot = valence_band[:, :, None] == jnp.arange(nval, dtype=jnp.int32)[None, None, :]
    con_hot = cond_band[:, :, None] == jnp.arange(ncon, dtype=jnp.int32)[None, None, :]
    low = jnp.sum(jnp.where(val_hot, valence_energy[None, None, :], 0.0), axis=2)
    high = jnp.sum(jnp.where(con_hot, cond_energy[None, None, :], 0.0), axis=2)
    low = low.reshape(nblk, 8, 2, 4).transpose(2, 1, 0, 3)
    delta = (high[None, None, :, None, :] - low[:, :, :, :, None]).reshape(1, -1)
    omega = 1.5 * jnp.arange(NFREQ).astype(jnp.float32)
    scale = 1.0 / jnp.sqrt(jnp.float32(delta.shape[1]))
    return -4.0 * delta / (delta**2 + omega[:, None] ** 2) * scale


def project_kernel(p_hbm, e_hbm, rows_out, cols_out, pairs, eig, total, landed, mid, mid_landed, halves, spread,
                   gather_send, gather_recv, copy_sem, eig_send, eig_recv, x_send, x_recv, y_send, y_recv,
                   spread_send, spread_recv, cols_send, cols_recv, rows_send, rows_recv, twin_send, twin_recv, local_sem):
    row, col = lax.axis_index("row"), lax.axis_index("col")
    core = lax.rem(col, 2)
    j = col // 2
    z, h = j // 2, lax.rem(j, 2)
    ylo, x = row // 4, lax.rem(row, 4)
    m_half = e_hbm.shape[0]
    source, mark = z // 2 == ylo, lax.rem(j, 4)
    place = lax.rem(z + 4 - 2 * ylo, 4)

    def seat(zz, hh, cc):
        return (row, zz * 4 + hh * 2 + cc)

    up = seat(lax.rem(z + 1, 4), h, core)
    down = seat(lax.rem(z + 3, 4), h, core)
    across = seat(z, 1 - h, core)
    twin = (row, col + 1 - 2 * core)

    block_rows = p_hbm.shape[1]
    local = [
        pltpu.make_async_copy(p_hbm.at[b], pairs.at[pl.ds(b * block_rows, block_rows)], copy_sem.at[b])
        for b in range(2)
    ]
    mine = pl.ds(pl.multiple_of(core * m_half, 16), m_half)
    local.append(pltpu.make_async_copy(e_hbm, eig.at[mine], copy_sem.at[2]))
    for c in local:
        c.start()

    barrier = pltpu.get_barrier_semaphore()

    def greet_rows(d, carry):
        other = ylo * 4 + lax.rem(x + d, 4)
        for c in range(2):
            pl.semaphore_signal(barrier, inc=1, device_id=(other, j * 2 + c), device_id_type=MESH)
        return carry

    def greet_cols(d, carry):
        other = lax.rem(j + d, 8)
        pl.semaphore_signal(barrier, inc=1, device_id=(row, other * 2 + core), device_id_type=MESH)
        return carry

    lax.fori_loop(1, 4, greet_rows, 0)
    lax.fori_loop(1, 8, greet_cols, 0)
    for other in (twin, ((1 - ylo) * 4 + x, col)):
        pl.semaphore_signal(barrier, inc=1, device_id=other, device_id_type=MESH)
    pl.semaphore_wait(barrier, 15)

    eig_copy = pltpu.make_async_remote_copy(
        e_hbm, eig.at[mine], eig_send, eig_recv, device_id=twin, device_id_type=MESH
    )

    a0, a1, a2 = 0, TA1 * LANE, (TA1 + TA2) * LANE
    b1, b2 = a2 + TB1 * LANE, a2 + (TB1 + TB2) * LANE
    piece = {"A": (a0, a2), "A1": (a0, a1), "A2": (a1, a2), "B": (a2, b2), "B1": (a2, b1), "B2": (b1, b2)}
    for name in ("A1", "A2"):
        lo, hi = piece[name]
        cut = lo + (hi - lo) // (2 * LANE) * LANE
        piece[name + "a"], piece[name + "b"] = (lo, cut), (cut, hi)

    slot_of = {(0, 0): 0, (0, 1): 1, (1, 0): 2, (3, 0): 3, (1, 1): 4, (3, 1): 5, (2, 0): 6, (2, 1): 7}
    place_of = {s: k for k, s in slot_of.items()}
    copies = {}
    begun = set()

    def region(slot, name):
        lo, hi = piece[name]
        return pairs.at[pl.ds(64 * slot, 64), pl.ds(lo, hi - lo)]

    def send(slot, name, way):
        dz, dh = place_of[slot]
        target, there = {
            "up": (up, ((dz + 3) % 4, dh)),
            "down": (down, ((dz + 1) % 4, dh)),
            "across": (across, (dz, 1 - dh)),
        }[way]
        there = slot_of[there]
        n = len(copies)
        c = pltpu.make_async_remote_copy(
            region(slot, name), region(there, name), gather_send.at[n], gather_recv.at[n],
            device_id=target, device_id_type=MESH,
        )
        copies[(there, name)] = c
        c.start()

    def arrive(slot, name):
        copies[(slot, name)].wait_recv()

    def multiply(first, last, name):
        lo, hi = piece[name]
        rows = pl.ds(64 * first, 64 * (last - first))
        value = lax.dot_general(
            pairs[rows, lo:hi], eig[:, lo:hi], (((1,), (1,)), ((), ())), preferred_element_type=jnp.float32
        )
        if first in begun:
            total[rows, :] += value
        else:
            total[rows, :] = value
        begun.update(range(first, last))

    def quarter(g):
        return pl.ds(sum(QUARTER[:g]), QUARTER[g])

    def pair_row(g, owner, jj, cc):
        if QUARTER[g] == 32:
            dz, dh, at = 1 + 2 * (owner // 2), g - 2, 32 * lax.rem(owner, 2)
        else:
            dz, dh, at = 2 * (g // 4), g % 2 if g < 2 else g - 4, 16 * owner
        zz = lax.rem(jj // 2 + dz, 4)
        hh = lax.rem(lax.rem(jj, 2) + dh, 2)
        return pl.multiple_of(cc * 512 + (zz * 2 + hh) * 64 + at, 16)

    def at_x(xx, cc):
        return (ylo * 4 + xx, j * 2 + cc)

    def own_rows(g, xx):
        return pl.ds(pl.multiple_of(GROUP[g] + xx * QUARTER[g], 16), QUARTER[g])

    def around(step):
        for d in (2, 1, 3):
            step(d, 0)

    def sum_x(g):
        def go(d, carry):
            to = lax.rem(x + d, 4)
            pltpu.make_async_remote_copy(
                total.at[own_rows(g, to)], landed.at[d - 1, quarter(g)], x_send.at[g], x_recv.at[g],
                device_id=at_x(to, core), device_id_type=MESH,
            ).start()
            return carry

        around(go)

    def y_copy(g):
        return pltpu.make_async_remote_copy(
            mid.at[quarter(g)], mid_landed.at[quarter(g)], y_send.at[g], y_recv.at[g],
            device_id=((1 - ylo) * 4 + x, col), device_id_type=MESH,
        )

    def sum_y(g):
        three = landed.at[:, quarter(g)]
        pltpu.make_async_copy(three, three, x_recv.at[g]).wait()
        value = total[own_rows(g, x), :]
        for d in range(3):
            value = value + landed[d, quarter(g), :]
        mid[quarter(g), :] = value
        y_copy(g).start()

    def spread_copy(g, k, zz, hh):
        block = spread.at[k, quarter(g)]
        return pltpu.make_async_remote_copy(
            block, block, spread_send, spread_recv.at[g, k], device_id=seat(zz, hh, core), device_id_type=MESH
        )

    def hand_rows(g):
        y_copy(g).wait_recv()
        value = (mid[quarter(g), :] + mid_landed[quarter(g), :]).astype(spread.dtype)

        @pl.when(source)
        def _():
            spread[mark, quarter(g), :] = value
            if g == NG - 1:
                spread_copy(g, mark, lax.rem(z + 2, 4), 1 - h).start()
                spread_copy(g, mark, lax.rem(z + 2, 4), h).start()
            for dz in (1, 3):
                spread_copy(g, mark, lax.rem(z + dz, 4), h).start()
            for dz in (1, 3):
                spread_copy(g, mark, lax.rem(z + dz, 4), 1 - h).start()
            spread_copy(g, mark, z, 1 - h).start()

        halves[0, quarter(g), :] = value[:, :m_half]
        halves[1, quarter(g), :] = value[:, m_half:]

    def spread_wait(g, k):
        block = spread.at[k, quarter(g)]
        pltpu.make_async_copy(block, block, spread_recv.at[g, k]).wait()

    def pass_z(g):
        @pl.when(place == 2)
        def _():
            for k in (2, 3):
                spread_wait(g, k)
                spread_copy(g, k, lax.rem(z + 1, 4), h).start()

        @pl.when(place == 3)
        def _():
            for k in (0, 1):
                spread_wait(g, k)
                spread_copy(g, k, lax.rem(z + 3, 4), h).start()

    def hand_cols(g):
        here = cols_out.at[pl.ds(pair_row(g, x, j, core), QUARTER[g])]

        def go_cols(d, carry):
            to = lax.rem(x + d, 4)
            for c in range(2):
                pltpu.make_async_remote_copy(
                    halves.at[c, quarter(g)], here, cols_send, cols_recv,
                    device_id=at_x(to, c), device_id_type=MESH,
                ).start()
            return carry

        around(go_cols)
        pltpu.make_async_remote_copy(
            halves.at[1 - core, quarter(g)], here, cols_send, cols_recv, device_id=twin, device_id_type=MESH
        ).start()
        pltpu.make_async_copy(halves.at[core, quarter(g)], here, local_sem.at[g]).start()

    def deal(g):
        for k in range(4):
            if g == NG - 1:
                pl.when(4 * ylo + k != j)(functools.partial(spread_wait, g, k))
            else:
                pl.when((4 * ylo + k != j) & (place != 3 - k // 2))(
                    functools.partial(spread_wait, g, k)
                )

        def there(to):
            return rows_out.at[pl.ds(pair_row(g, x, 4 * ylo + to, core), QUARTER[g])]

        def go(d, carry):
            to = lax.rem(x + d, 4)
            pltpu.make_async_remote_copy(
                spread.at[to, quarter(g)], there(to), rows_send, rows_recv.at[g],
                device_id=at_x(to, core), device_id_type=MESH,
            ).start()
            if g in BOTH:
                pltpu.make_async_remote_copy(
                    spread.at[to, quarter(g)], there(to), twin_send, twin_recv,
                    device_id=at_x(to, 1 - core), device_id_type=MESH,
                ).start()
            return carry

        around(go)
        kept = spread.at[x, quarter(g)]
        pltpu.make_async_copy(kept, there(x), local_sem.at[NG + g]).start()
        pltpu.make_async_remote_copy(
            kept, there(x), twin_send, twin_recv, device_id=twin, device_id_type=MESH
        ).start()

    def arrived(g):
        three = rows_out.at[pl.ds(0, 3 * QUARTER[g])]
        pltpu.make_async_copy(three, three, rows_recv.at[g]).wait()

    def pass_on(g):
        arrived(g)

        def go(d, carry):
            block = rows_out.at[pl.ds(pair_row(g, lax.rem(x + d, 4), row, core), QUARTER[g])]
            pltpu.make_async_remote_copy(
                block, block, twin_send, twin_recv, device_id=twin, device_id_type=MESH
            ).start()
            return carry

        around(go)

    local[0].wait()
    local[1].wait()
    send(0, "B", "up")
    send(0, "B", "down")
    send(0, "A", "across")
    eig_copy.start()
    send(0, "A", "up")
    send(0, "A", "down")
    send(0, "B", "across")
    local[2].wait()
    eig_copy.wait()
    multiply(0, 1, "B")
    multiply(0, 1, "A")
    sum_x(0)
    arrive(3, "B")
    send(3, "B1", "up")
    arrive(2, "B")
    send(2, "B2", "down")
    sum_y(0)
    send(3, "B", "across")
    send(2, "B", "across")
    arrive(1, "A")
    send(1, "A", "up")
    send(1, "A", "down")
    arrive(3, "A")
    send(3, "A1", "up")
    arrive(2, "A")
    send(2, "A2", "down")
    multiply(1, 4, "A")
    arrive(1, "B")
    multiply(1, 4, "B")
    sum_x(1)
    sum_x(2)
    arrive(6, "B1")
    arrive(6, "B2")
    multiply(6, 7, "B")
    sum_y(1)
    sum_y(2)
    send(6, "B1", "across")
    send(6, "B2", "across")
    arrive(5, "A")
    send(5, "A1a", "up")
    send(5, "A1b", "up")
    arrive(4, "A")
    send(4, "A2a", "down")
    send(4, "A2b", "down")
    hand_rows(0)
    hand_cols(0)
    arrive(5, "B")
    arrive(4, "B")
    multiply(4, 6, "B")
    multiply(4, 6, "A")
    sum_x(3)
    hand_rows(1)
    hand_rows(2)
    hand_cols(1)
    hand_cols(2)
    arrive(6, "A1")
    arrive(6, "A2")
    multiply(6, 7, "A")
    sum_x(4)
    arrive(7, "A1a")
    multiply(7, 8, "A1a")
    arrive(7, "A2a")
    multiply(7, 8, "A2a")
    arrive(7, "B1")
    arrive(7, "B2")
    multiply(7, 8, "B")
    arrive(7, "A1b")
    multiply(7, 8, "A1b")
    arrive(7, "A2b")
    multiply(7, 8, "A2b")
    sum_x(5)
    sum_y(3)
    sum_y(4)
    pass_z(0)
    pass_z(1)
    pass_z(2)
    hand_rows(3)
    sum_y(5)
    hand_rows(4)
    hand_cols(3)
    hand_cols(4)
    deal(0)
    deal(1)
    deal(2)
    hand_rows(5)
    hand_cols(5)
    pass_z(3)
    pass_z(4)
    deal(3)
    deal(4)
    pass_on(0)
    pass_on(1)
    pass_on(2)
    pass_on(3)
    pass_on(4)
    deal(5)
    arrived(5)

    for c in copies.values():
        c.wait_send()
    for g in range(NG):
        three = landed.at[:, quarter(g)]
        pltpu.make_async_copy(three, three, x_send.at[g]).wait()
        y_copy(g).wait_send()
        for n, block in ((g, cols_out.at[pl.ds(0, QUARTER[g])]), (NG + g, rows_out.at[pl.ds(0, QUARTER[g])])):
            pltpu.make_async_copy(block, block, local_sem.at[n]).wait()

    def wait_rows(ref, count, s):
        block = ref.at[pl.ds(0, count)]
        pltpu.make_async_copy(block, block, s).wait()

    mine = sum(QUARTER)

    @pl.when(source)
    def _():
        wait_rows(rows_out, 5 * mine + 2 * QUARTER[NG - 1], spread_send)

    @pl.when(place >= 2)
    def _():
        wait_rows(rows_out, 2 * (mine - QUARTER[NG - 1]), spread_send)

    wait_rows(cols_out, 7 * mine, cols_send)
    wait_rows(cols_out, 7 * mine, cols_recv)
    wait_rows(rows_out, 3 * mine, rows_send)
    wait_rows(rows_out, 4 * mine, twin_send)
    wait_rows(rows_out, 4 * mine, twin_recv)


def project(pairs_t, eig_t):
    nblk, pair_rows, depth = pairs_t.shape
    m_half = eig_t.shape[0]
    m_all = 2 * m_half
    bf16, f32 = jnp.bfloat16, jnp.float32
    dma = pltpu.SemaphoreType.DMA
    mine = sum(QUARTER)
    return pl.pallas_call(
        project_kernel,
        out_shape=(
            jax.ShapeDtypeStruct((1024, m_all), bf16),
            jax.ShapeDtypeStruct((1024, m_half), bf16),
        ),
        in_specs=[pl.BlockSpec(memory_space=pltpu.HBM)] * 2,
        out_specs=(pl.BlockSpec(memory_space=pl.ANY),) * 2,
        scratch_shapes=[
            pltpu.VMEM((512, depth), bf16),
            pltpu.VMEM((m_all, depth), bf16),
            pltpu.VMEM((512, m_all), f32),
            pltpu.VMEM((3, mine, m_all), f32),
            pltpu.VMEM((mine, m_all), f32),
            pltpu.VMEM((mine, m_all), f32),
            pltpu.VMEM((2, mine, m_half), bf16),
            pltpu.VMEM((4, mine, m_all), bf16),
            dma((20,)), dma((20,)), dma((3,)), dma, dma, dma((NG,)), dma((NG,)), dma((NG,)), dma((NG,)),
            dma, dma((NG, 4)), dma, dma, dma, dma((NG,)), dma, dma, dma((2 * NG,)),
        ],
        compiler_params=pltpu.CompilerParams(
            collective_id=0, has_side_effects=True, vmem_limit_bytes=48 * 2**20
        ),
        name="project",
    )(*(pltpu.with_memory_space_constraint(a, pltpu.HBM) for a in (pairs_t, eig_t)))


def chi_kernel(factor_ref, rows_ref, cols_ref, out_ref, cols_t, scaled):
    @pl.when(pl.program_id(0) == 0)
    def _():
        cols_t[...] = cols_ref[...].astype(jnp.float32).T

    s_cols = cols_t.shape[0]
    for w in range(STEP):
        scaled[w * s_cols:(w + 1) * s_cols] = (
            cols_t[...] * factor_ref[pl.ds(pl.program_id(0) * STEP + w, 1), :]
        ).astype(scaled.dtype)
    value = jnp.dot(scaled[...], rows_ref[...], preferred_element_type=jnp.float32)
    out_ref[...] = value.reshape(out_ref.shape)


def polarizability(factor, rows, cols):
    n, s_rows = rows.shape
    s_cols = cols.shape[1]
    return pl.pallas_call(
        chi_kernel,
        grid=(NFREQ // STEP,),
        out_shape=jax.ShapeDtypeStruct((NFREQ, s_cols, s_rows), jnp.float32),
        in_specs=[
            pl.BlockSpec((NFREQ, n), lambda w: (0, 0)),
            pl.BlockSpec((n, s_rows), lambda w: (0, 0)),
            pl.BlockSpec((n, s_cols), lambda w: (0, 0)),
        ],
        out_specs=pl.BlockSpec((STEP, s_cols, s_rows), lambda w: (w, 0, 0)),
        scratch_shapes=[pltpu.VMEM((s_cols, n), jnp.float32), pltpu.VMEM((STEP * s_cols, n), jnp.bfloat16)],
        compiler_params=pltpu.CompilerParams(vmem_limit_bytes=32 * 2**20),
        name="chi",
    )(factor, rows, cols)


def local(pair_products, eigvecs, valence_band, cond_band, valence_energy, cond_energy):
    factor = pair_factor(valence_band, cond_band, valence_energy, cond_energy)
    rows, cols = project(pair_products.transpose(0, 2, 1), eigvecs.T)
    return polarizability(factor, rows, cols).transpose(0, 2, 1)


def solution(mesh):
    return jax.shard_map(
        local,
        mesh=mesh,
        in_specs=(P(None, "row", "col"), P("row", "col"), P(), P(), P(), P()),
        out_specs=P(None, "row", "col"),
        check_vma=False,
    )
```

```python
import functools

import jax
import jax.numpy as jnp
from jax import lax
from jax.experimental import pallas as pl
from jax.experimental.pallas import tpu as pltpu
from jax.sharding import PartitionSpec as P

NFREQ = 12
STEP = 3
MESH = pl.DeviceIdType.MESH
LANE = 128
TA1, TA2, TB1, TB2 = 14, 14, 9, 8
GROUP = (0, 64, 128, 256, 384, 448)
QUARTER = (16, 16, 32, 32, 16, 16)
NG = len(GROUP)
FAR = (3, 4, 5)
BOTH = (3, 4, 5)


def project_kernel(p_hbm, e_hbm, vband_hbm, cband_hbm, venergy_hbm, cenergy_hbm, rows_out, cols_out, factor_out,
                   pairs, eig, total, landed, mid, mid_landed, halves, spread,
                   gather_send, gather_recv, copy_sem, eig_send, eig_recv, x_send, x_recv, y_send, y_recv,
                   spread_send, spread_recv, cols_send, cols_recv, rows_send, rows_recv, twin_send, twin_recv, local_sem,
                   vband, cband, venergy, cenergy, factors, table_sem, factor_sem):
    row, col = lax.axis_index("row"), lax.axis_index("col")
    core = lax.rem(col, 2)
    j = col // 2
    z, h = j // 2, lax.rem(j, 2)
    ylo, x = row // 4, lax.rem(row, 4)
    m_half = e_hbm.shape[0]
    source, mark = z // 2 == ylo, lax.rem(j, 4)
    place = lax.rem(z + 4 - 2 * ylo, 4)

    def seat(zz, hh, cc):
        return (row, zz * 4 + hh * 2 + cc)

    up = seat(lax.rem(z + 1, 4), h, core)
    down = seat(lax.rem(z + 3, 4), h, core)
    across = seat(z, 1 - h, core)
    twin = (row, col + 1 - 2 * core)

    block_rows = p_hbm.shape[1]
    local = [
        pltpu.make_async_copy(p_hbm.at[b], pairs.at[pl.ds(b * block_rows, block_rows)], copy_sem.at[b])
        for b in range(2)
    ]
    mine = pl.ds(pl.multiple_of(core * m_half, 16), m_half)
    local.append(pltpu.make_async_copy(e_hbm, eig.at[mine], copy_sem.at[2]))
    for c in local:
        c.start()

    tables = [
        pltpu.make_async_copy(src, dst, table_sem.at[n])
        for n, (src, dst) in enumerate(
            ((vband_hbm, vband), (cband_hbm, cband), (venergy_hbm, venergy), (cenergy_hbm, cenergy))
        )
    ]
    for c in tables:
        c.start()

    barrier = pltpu.get_barrier_semaphore()

    def greet_rows(d, carry):
        other = ylo * 4 + lax.rem(x + d, 4)
        for c in range(2):
            pl.semaphore_signal(barrier, inc=1, device_id=(other, j * 2 + c), device_id_type=MESH)
        return carry

    def greet_cols(d, carry):
        other = lax.rem(j + d, 8)
        pl.semaphore_signal(barrier, inc=1, device_id=(row, other * 2 + core), device_id_type=MESH)
        return carry

    lax.fori_loop(1, 4, greet_rows, 0)
    lax.fori_loop(1, 8, greet_cols, 0)
    for other in (twin, ((1 - ylo) * 4 + x, col)):
        pl.semaphore_signal(barrier, inc=1, device_id=other, device_id_type=MESH)
    pl.semaphore_wait(barrier, 15)

    eig_copy = pltpu.make_async_remote_copy(
        e_hbm, eig.at[mine], eig_send, eig_recv, device_id=twin, device_id_type=MESH
    )

    a0, a1, a2 = 0, TA1 * LANE, (TA1 + TA2) * LANE
    b1, b2 = a2 + TB1 * LANE, a2 + (TB1 + TB2) * LANE
    piece = {"A": (a0, a2), "A1": (a0, a1), "A2": (a1, a2), "B": (a2, b2), "B1": (a2, b1), "B2": (b1, b2)}
    for name in ("A1", "A2"):
        lo, hi = piece[name]
        cut = lo + (hi - lo) // (2 * LANE) * LANE
        piece[name + "a"], piece[name + "b"] = (lo, cut), (cut, hi)

    slot_of = {(0, 0): 0, (0, 1): 1, (1, 0): 2, (3, 0): 3, (1, 1): 4, (3, 1): 5, (2, 0): 6, (2, 1): 7}
    place_of = {s: k for k, s in slot_of.items()}
    copies = {}
    begun = set()

    def region(slot, name):
        lo, hi = piece[name]
        return pairs.at[pl.ds(64 * slot, 64), pl.ds(lo, hi - lo)]

    def send(slot, name, way):
        dz, dh = place_of[slot]
        target, there = {
            "up": (up, ((dz + 3) % 4, dh)),
            "down": (down, ((dz + 1) % 4, dh)),
            "across": (across, (dz, 1 - dh)),
        }[way]
        there = slot_of[there]
        n = len(copies)
        c = pltpu.make_async_remote_copy(
            region(slot, name), region(there, name), gather_send.at[n], gather_recv.at[n],
            device_id=target, device_id_type=MESH,
        )
        copies[(there, name)] = c
        c.start()

    def arrive(slot, name):
        copies[(slot, name)].wait_recv()

    def multiply(first, last, name):
        lo, hi = piece[name]
        rows = pl.ds(64 * first, 64 * (last - first))
        value = lax.dot_general(
            pairs[rows, lo:hi], eig[:, lo:hi], (((1,), (1,)), ((), ())), preferred_element_type=jnp.float32
        )
        if first in begun:
            total[rows, :] += value
        else:
            total[rows, :] = value
        begun.update(range(first, last))

    def quarter(g):
        return pl.ds(sum(QUARTER[:g]), QUARTER[g])

    def pair_row(g, owner, jj, cc):
        if QUARTER[g] == 32:
            dz, dh, at = 1 + 2 * (owner // 2), g - 2, 32 * lax.rem(owner, 2)
        else:
            dz, dh, at = 2 * (g // 4), g % 2 if g < 2 else g - 4, 16 * owner
        zz = lax.rem(jj // 2 + dz, 4)
        hh = lax.rem(lax.rem(jj, 2) + dh, 2)
        return pl.multiple_of(cc * 512 + (zz * 2 + hh) * 64 + at, 16)

    def at_x(xx, cc):
        return (ylo * 4 + xx, j * 2 + cc)

    def own_rows(g, xx):
        return pl.ds(pl.multiple_of(GROUP[g] + xx * QUARTER[g], 16), QUARTER[g])

    def pair_factors():
        for c in tables:
            c.wait()
        nblk, nv = vband.shape
        nc = cband.shape[1]
        part_of = lax.broadcasted_iota(jnp.int32, (8, LANE), 0)
        lane = lax.broadcasted_iota(jnp.int32, (8, LANE), 1)
        blk = (lane // 32) % 2
        v_of = blk * nv + ((part_of % 4) * 2 + lane // 64) * 8 + (part_of // 4) * 4 + (lane % 32) // 8
        c_of = blk * nc + lane % 8

        def valence(i, low):
            for n in range(4):
                i4 = i * 4 + n
                low = jnp.where(v_of == i4, venergy[vband[i4 // nv, i4 % nv]], low)
            return low

        def conduction(i, high):
            return jnp.where(c_of == i, cenergy[cband[i // nc, i % nc]], high)

        low = lax.fori_loop(0, nblk * nv // 4, valence, jnp.zeros((8, LANE), jnp.float32))
        high = lax.fori_loop(0, nblk * nc, conduction, jnp.zeros((8, LANE), jnp.float32))
        delta = high - low
        scale = 1.0 / (8 * LANE) ** 0.5
        for w in range(NFREQ):
            value = -4.0 * delta / (delta * delta + (1.5 * w) ** 2) * scale
            for n in range(8):
                factors[w:w + 1, n * LANE:(n + 1) * LANE] = value[n:n + 1, :]
        pltpu.make_async_copy(factors, factor_out, factor_sem).start()

    def around(step):
        for d in (2, 1, 3):
            step(d, 0)

    def sum_x(g):
        def go(d, carry):
            to = lax.rem(x + d, 4)
            pltpu.make_async_remote_copy(
                total.at[own_rows(g, to)], landed.at[d - 1, quarter(g)], x_send.at[g], x_recv.at[g],
                device_id=at_x(to, core), device_id_type=MESH,
            ).start()
            return carry

        around(go)

    def y_copy(g):
        return pltpu.make_async_remote_copy(
            mid.at[quarter(g)], mid_landed.at[quarter(g)], y_send.at[g], y_recv.at[g],
            device_id=((1 - ylo) * 4 + x, col), device_id_type=MESH,
        )

    def sum_y(g):
        three = landed.at[:, quarter(g)]
        pltpu.make_async_copy(three, three, x_recv.at[g]).wait()
        value = total[own_rows(g, x), :]
        for d in range(3):
            value = value + landed[d, quarter(g), :]
        mid[quarter(g), :] = value
        y_copy(g).start()

    def spread_copy(g, k, zz, hh):
        block = spread.at[k, quarter(g)]
        return pltpu.make_async_remote_copy(
            block, block, spread_send, spread_recv.at[g, k], device_id=seat(zz, hh, core), device_id_type=MESH
        )

    def hand_rows(g):
        y_copy(g).wait_recv()
        value = (mid[quarter(g), :] + mid_landed[quarter(g), :]).astype(spread.dtype)

        @pl.when(source)
        def _():
            spread[mark, quarter(g), :] = value
            if g in FAR:
                spread_copy(g, mark, lax.rem(z + 2, 4), 1 - h).start()
                spread_copy(g, mark, lax.rem(z + 2, 4), h).start()
            for dz in (1, 3):
                spread_copy(g, mark, lax.rem(z + dz, 4), h).start()
            for dz in (1, 3):
                spread_copy(g, mark, lax.rem(z + dz, 4), 1 - h).start()
            spread_copy(g, mark, z, 1 - h).start()

        halves[0, quarter(g), :] = value[:, :m_half]
        halves[1, quarter(g), :] = value[:, m_half:]

    def spread_wait(g, k):
        block = spread.at[k, quarter(g)]
        pltpu.make_async_copy(block, block, spread_recv.at[g, k]).wait()

    def pass_z(g):
        @pl.when(place == 2)
        def _():
            for k in (2, 3):
                spread_wait(g, k)
                spread_copy(g, k, lax.rem(z + 1, 4), h).start()

        @pl.when(place == 3)
        def _():
            for k in (0, 1):
                spread_wait(g, k)
                spread_copy(g, k, lax.rem(z + 3, 4), h).start()

    def hand_cols(g):
        here = cols_out.at[pl.ds(pair_row(g, x, j, core), QUARTER[g])]

        def go_cols(d, carry):
            to = lax.rem(x + d, 4)
            for c in range(2):
                pltpu.make_async_remote_copy(
                    halves.at[c, quarter(g)], here, cols_send, cols_recv,
                    device_id=at_x(to, c), device_id_type=MESH,
                ).start()
            return carry

        around(go_cols)
        pltpu.make_async_remote_copy(
            halves.at[1 - core, quarter(g)], here, cols_send, cols_recv, device_id=twin, device_id_type=MESH
        ).start()
        pltpu.make_async_copy(halves.at[core, quarter(g)], here, local_sem.at[g]).start()

    def deal(g):
        for k in range(4):
            if g in FAR:
                pl.when(4 * ylo + k != j)(functools.partial(spread_wait, g, k))
            else:
                pl.when((4 * ylo + k != j) & (place != 3 - k // 2))(
                    functools.partial(spread_wait, g, k)
                )

        def there(to):
            return rows_out.at[pl.ds(pair_row(g, x, 4 * ylo + to, core), QUARTER[g])]

        def go(d, carry):
            to = lax.rem(x + d, 4)
            pltpu.make_async_remote_copy(
                spread.at[to, quarter(g)], there(to), rows_send, rows_recv.at[g],
                device_id=at_x(to, core), device_id_type=MESH,
            ).start()
            if g in BOTH:
                pltpu.make_async_remote_copy(
                    spread.at[to, quarter(g)], there(to), twin_send, twin_recv,
                    device_id=at_x(to, 1 - core), device_id_type=MESH,
                ).start()
            return carry

        around(go)
        kept = spread.at[x, quarter(g)]
        pltpu.make_async_copy(kept, there(x), local_sem.at[NG + g]).start()
        pltpu.make_async_remote_copy(
            kept, there(x), twin_send, twin_recv, device_id=twin, device_id_type=MESH
        ).start()

    def arrived(g):
        three = rows_out.at[pl.ds(0, 3 * QUARTER[g])]
        pltpu.make_async_copy(three, three, rows_recv.at[g]).wait()

    def pass_on(g):
        arrived(g)

        def go(d, carry):
            block = rows_out.at[pl.ds(pair_row(g, lax.rem(x + d, 4), row, core), QUARTER[g])]
            pltpu.make_async_remote_copy(
                block, block, twin_send, twin_recv, device_id=twin, device_id_type=MESH
            ).start()
            return carry

        around(go)

    local[0].wait()
    local[1].wait()
    send(0, "B", "up")
    send(0, "B", "down")
    send(0, "A", "across")
    eig_copy.start()
    send(0, "A", "up")
    send(0, "A", "down")
    send(0, "B", "across")
    pair_factors()
    local[2].wait()
    eig_copy.wait()
    multiply(0, 1, "B")
    multiply(0, 1, "A")
    sum_x(0)
    arrive(3, "B")
    send(3, "B1", "up")
    arrive(2, "B")
    send(2, "B2", "down")
    sum_y(0)
    send(3, "B", "across")
    send(2, "B", "across")
    arrive(1, "A")
    send(1, "A", "up")
    send(1, "A", "down")
    arrive(3, "A")
    send(3, "A1", "up")
    arrive(2, "A")
    send(2, "A2", "down")
    multiply(1, 4, "A")
    arrive(1, "B")
    multiply(1, 4, "B")
    sum_x(1)
    sum_x(2)
    arrive(6, "B1")
    arrive(6, "B2")
    multiply(6, 7, "B")
    sum_y(1)
    sum_y(2)
    send(6, "B1", "across")
    send(6, "B2", "across")
    arrive(5, "A")
    send(5, "A1a", "up")
    send(5, "A1b", "up")
    arrive(4, "A")
    send(4, "A2a", "down")
    send(4, "A2b", "down")
    hand_rows(0)
    hand_cols(0)
    arrive(5, "B")
    arrive(4, "B")
    multiply(4, 6, "B")
    multiply(4, 6, "A")
    sum_x(3)
    hand_rows(1)
    hand_rows(2)
    hand_cols(1)
    hand_cols(2)
    arrive(6, "A1")
    arrive(6, "A2")
    multiply(6, 7, "A")
    sum_x(4)
    arrive(7, "A1a")
    multiply(7, 8, "A1a")
    arrive(7, "A2a")
    multiply(7, 8, "A2a")
    arrive(7, "B1")
    arrive(7, "B2")
    multiply(7, 8, "B")
    arrive(7, "A1b")
    multiply(7, 8, "A1b")
    arrive(7, "A2b")
    multiply(7, 8, "A2b")
    sum_x(5)
    sum_y(3)
    sum_y(4)
    pass_z(0)
    pass_z(1)
    pass_z(2)
    hand_rows(3)
    sum_y(5)
    hand_rows(4)
    hand_cols(3)
    hand_cols(4)
    deal(0)
    deal(1)
    deal(2)
    hand_rows(5)
    hand_cols(5)
    deal(3)
    deal(4)
    deal(5)
    pass_on(0)
    pass_on(1)
    pass_on(2)
    arrived(3)
    arrived(4)
    arrived(5)

    pltpu.make_async_copy(factors, factor_out, factor_sem).wait()
    for c in copies.values():
        c.wait_send()
    for g in range(NG):
        three = landed.at[:, quarter(g)]
        pltpu.make_async_copy(three, three, x_send.at[g]).wait()
        y_copy(g).wait_send()
        for n, block in ((g, cols_out.at[pl.ds(0, QUARTER[g])]), (NG + g, rows_out.at[pl.ds(0, QUARTER[g])])):
            pltpu.make_async_copy(block, block, local_sem.at[n]).wait()

    def wait_rows(ref, count, s):
        block = ref.at[pl.ds(0, count)]
        pltpu.make_async_copy(block, block, s).wait()

    mine, far = sum(QUARTER), sum(QUARTER[g] for g in FAR)

    @pl.when(source)
    def _():
        wait_rows(rows_out, 5 * mine + 2 * far, spread_send)

    @pl.when(place >= 2)
    def _():
        wait_rows(rows_out, 2 * (mine - far), spread_send)

    wait_rows(cols_out, 7 * mine, cols_send)
    wait_rows(cols_out, 7 * mine, cols_recv)
    wait_rows(rows_out, 3 * mine, rows_send)
    wait_rows(rows_out, 4 * mine, twin_send)
    wait_rows(rows_out, 4 * mine, twin_recv)


def project(pairs_t, eig_t, *tables):
    nblk, pair_rows, depth = pairs_t.shape
    m_half = eig_t.shape[0]
    m_all = 2 * m_half
    bf16, f32 = jnp.bfloat16, jnp.float32
    dma = pltpu.SemaphoreType.DMA
    mine = sum(QUARTER)
    return pl.pallas_call(
        project_kernel,
        out_shape=(
            jax.ShapeDtypeStruct((1024, m_all), bf16),
            jax.ShapeDtypeStruct((1024, m_half), bf16),
            jax.ShapeDtypeStruct((NFREQ, 1024), f32),
        ),
        in_specs=[pl.BlockSpec(memory_space=pltpu.HBM)] * 6,
        out_specs=(pl.BlockSpec(memory_space=pl.ANY),) * 3,
        scratch_shapes=[
            pltpu.VMEM((512, depth), bf16),
            pltpu.VMEM((m_all, depth), bf16),
            pltpu.VMEM((512, m_all), f32),
            pltpu.VMEM((3, mine, m_all), f32),
            pltpu.VMEM((mine, m_all), f32),
            pltpu.VMEM((mine, m_all), f32),
            pltpu.VMEM((2, mine, m_half), bf16),
            pltpu.VMEM((4, mine, m_all), bf16),
            dma((20,)), dma((20,)), dma((3,)), dma, dma, dma((NG,)), dma((NG,)), dma((NG,)), dma((NG,)),
            dma, dma((NG, 4)), dma, dma, dma, dma((NG,)), dma, dma, dma((2 * NG,)),
            *(pltpu.SMEM(a.shape, a.dtype) for a in tables), pltpu.VMEM((NFREQ, 1024), f32), dma((4,)), dma,
        ],
        compiler_params=pltpu.CompilerParams(
            collective_id=0, has_side_effects=True, vmem_limit_bytes=48 * 2**20
        ),
        name="project",
    )(*(pltpu.with_memory_space_constraint(a, pltpu.HBM) for a in (pairs_t, eig_t, *tables)))


def chi_kernel(factor_ref, rows_ref, cols_ref, out_ref, cols_t, scaled):
    @pl.when(pl.program_id(0) == 0)
    def _():
        cols_t[...] = cols_ref[...].T

    s_cols = cols_t.shape[0]
    for w in range(STEP):
        scaled[w * s_cols:(w + 1) * s_cols] = (
            cols_t[...].astype(jnp.float32) * factor_ref[pl.ds(pl.program_id(0) * STEP + w, 1), :]
        ).astype(scaled.dtype)
    value = jnp.dot(scaled[...], rows_ref[...], preferred_element_type=jnp.float32)
    out_ref[...] = value.reshape(out_ref.shape)


def polarizability(factor, rows, cols):
    n, s_rows = rows.shape
    s_cols = cols.shape[1]
    return pl.pallas_call(
        chi_kernel,
        grid=(NFREQ // STEP,),
        out_shape=jax.ShapeDtypeStruct((NFREQ, s_cols, s_rows), jnp.float32),
        in_specs=[pl.BlockSpec(memory_space=pltpu.VMEM)] * 3,
        out_specs=pl.BlockSpec((STEP, s_cols, s_rows), lambda w: (w, 0, 0)),
        scratch_shapes=[pltpu.VMEM((s_cols, n), jnp.bfloat16), pltpu.VMEM((STEP * s_cols, n), jnp.bfloat16)],
        compiler_params=pltpu.CompilerParams(vmem_limit_bytes=32 * 2**20),
        name="chi",
    )(factor, rows, cols)


def local(pair_products, eigvecs, valence_band, cond_band, valence_energy, cond_energy):
    rows, cols, factor = project(
        pair_products.transpose(0, 2, 1), eigvecs.T, valence_band, cond_band, valence_energy, cond_energy
    )
    return polarizability(factor, rows, cols).transpose(0, 2, 1)


def solution(mesh):
    return jax.shard_map(
        local,
        mesh=mesh,
        in_specs=(P(None, "row", "col"), P("row", "col"), P(), P(), P(), P()),
        out_specs=P(None, "row", "col"),
        check_vma=False,
    )
```

```python
import functools

import jax
import jax.numpy as jnp
from jax import lax
from jax.experimental import pallas as pl
from jax.experimental.pallas import tpu as pltpu
from jax.sharding import PartitionSpec as P

NFREQ = 12
STEP = 3
MESH = pl.DeviceIdType.MESH
LANE = 128
TA1, TA2, TB1, TB2 = 14, 14, 9, 8
GROUP = (0, 64, 128, 256, 384, 448)
QUARTER = (16, 16, 32, 32, 16, 16)
NG = len(GROUP)
FAR = (3, 4, 5)
BOTH = (5,)


def project_kernel(p_hbm, e_hbm, vband_hbm, cband_hbm, venergy_hbm, cenergy_hbm, rows_out, cols_out, factor_out,
                   pairs, eig, total, landed, mid, mid_landed, halves, spread,
                   gather_send, gather_recv, copy_sem, eig_send, eig_recv, x_send, x_recv, y_send, y_recv,
                   spread_send, spread_recv, cols_send, cols_recv, rows_send, rows_recv, twin_send, twin_recv, local_sem,
                   vband, cband, venergy, cenergy, factors, table_sem, factor_sem):
    row, col = lax.axis_index("row"), lax.axis_index("col")
    core = lax.rem(col, 2)
    j = col // 2
    z, h = j // 2, lax.rem(j, 2)
    ylo, x = row // 4, lax.rem(row, 4)
    m_half = e_hbm.shape[0]
    source, mark = z // 2 == ylo, lax.rem(j, 4)
    place = lax.rem(z + 4 - 2 * ylo, 4)

    def seat(zz, hh, cc):
        return (row, zz * 4 + hh * 2 + cc)

    up = seat(lax.rem(z + 1, 4), h, core)
    down = seat(lax.rem(z + 3, 4), h, core)
    across = seat(z, 1 - h, core)
    twin = (row, col + 1 - 2 * core)

    block_rows = p_hbm.shape[1]
    local = [
        pltpu.make_async_copy(p_hbm.at[b], pairs.at[pl.ds(b * block_rows, block_rows)], copy_sem.at[b])
        for b in range(2)
    ]
    mine = pl.ds(pl.multiple_of(core * m_half, 16), m_half)
    local.append(pltpu.make_async_copy(e_hbm, eig.at[mine], copy_sem.at[2]))
    for c in local:
        c.start()

    tables = [
        pltpu.make_async_copy(src, dst, table_sem.at[n])
        for n, (src, dst) in enumerate(
            ((vband_hbm, vband), (cband_hbm, cband), (venergy_hbm, venergy), (cenergy_hbm, cenergy))
        )
    ]
    for c in tables:
        c.start()

    barrier = pltpu.get_barrier_semaphore()

    def greet_rows(d, carry):
        other = ylo * 4 + lax.rem(x + d, 4)
        for c in range(2):
            pl.semaphore_signal(barrier, inc=1, device_id=(other, j * 2 + c), device_id_type=MESH)
        return carry

    def greet_cols(d, carry):
        other = lax.rem(j + d, 8)
        pl.semaphore_signal(barrier, inc=1, device_id=(row, other * 2 + core), device_id_type=MESH)
        return carry

    lax.fori_loop(1, 4, greet_rows, 0)
    lax.fori_loop(1, 8, greet_cols, 0)
    for other in (twin, ((1 - ylo) * 4 + x, col)):
        pl.semaphore_signal(barrier, inc=1, device_id=other, device_id_type=MESH)
    pl.semaphore_wait(barrier, 15)

    eig_copy = pltpu.make_async_remote_copy(
        e_hbm, eig.at[mine], eig_send, eig_recv, device_id=twin, device_id_type=MESH
    )

    a0, a1, a2 = 0, TA1 * LANE, (TA1 + TA2) * LANE
    b1, b2 = a2 + TB1 * LANE, a2 + (TB1 + TB2) * LANE
    piece = {"A": (a0, a2), "A1": (a0, a1), "A2": (a1, a2), "B": (a2, b2), "B1": (a2, b1), "B2": (b1, b2)}
    for name in ("A1", "A2"):
        lo, hi = piece[name]
        cut = lo + (hi - lo) // (2 * LANE) * LANE
        piece[name + "a"], piece[name + "b"] = (lo, cut), (cut, hi)

    slot_of = {(0, 0): 0, (0, 1): 1, (1, 0): 2, (3, 0): 3, (1, 1): 4, (3, 1): 5, (2, 0): 6, (2, 1): 7}
    place_of = {s: k for k, s in slot_of.items()}
    copies = {}
    begun = set()

    def region(slot, name):
        lo, hi = piece[name]
        return pairs.at[pl.ds(64 * slot, 64), pl.ds(lo, hi - lo)]

    def send(slot, name, way):
        dz, dh = place_of[slot]
        target, there = {
            "up": (up, ((dz + 3) % 4, dh)),
            "down": (down, ((dz + 1) % 4, dh)),
            "across": (across, (dz, 1 - dh)),
        }[way]
        there = slot_of[there]
        n = len(copies)
        c = pltpu.make_async_remote_copy(
            region(slot, name), region(there, name), gather_send.at[n], gather_recv.at[n],
            device_id=target, device_id_type=MESH,
        )
        copies[(there, name)] = c
        c.start()

    def arrive(slot, name):
        copies[(slot, name)].wait_recv()

    def multiply(first, last, name):
        lo, hi = piece[name]
        rows = pl.ds(64 * first, 64 * (last - first))
        value = lax.dot_general(
            pairs[rows, lo:hi], eig[:, lo:hi], (((1,), (1,)), ((), ())), preferred_element_type=jnp.float32
        )
        if first in begun:
            total[rows, :] += value
        else:
            total[rows, :] = value
        begun.update(range(first, last))

    def quarter(g):
        return pl.ds(sum(QUARTER[:g]), QUARTER[g])

    def pair_row(g, owner, jj, cc):
        if QUARTER[g] == 32:
            dz, dh, at = 1 + 2 * (owner // 2), g - 2, 32 * lax.rem(owner, 2)
        else:
            dz, dh, at = 2 * (g // 4), g % 2 if g < 2 else g - 4, 16 * owner
        zz = lax.rem(jj // 2 + dz, 4)
        hh = lax.rem(lax.rem(jj, 2) + dh, 2)
        return pl.multiple_of(cc * 512 + (zz * 2 + hh) * 64 + at, 16)

    def at_x(xx, cc):
        return (ylo * 4 + xx, j * 2 + cc)

    def own_rows(g, xx):
        return pl.ds(pl.multiple_of(GROUP[g] + xx * QUARTER[g], 16), QUARTER[g])

    def pair_factors():
        for c in tables:
            c.wait()
        nblk, nv = vband.shape
        nc = cband.shape[1]
        part_of = lax.broadcasted_iota(jnp.int32, (8, LANE), 0)
        lane = lax.broadcasted_iota(jnp.int32, (8, LANE), 1)
        blk = (lane // 32) % 2
        v_of = blk * nv + ((part_of % 4) * 2 + lane // 64) * 8 + (part_of // 4) * 4 + (lane % 32) // 8
        c_of = blk * nc + lane % 8

        def valence(i, low):
            for n in range(4):
                i4 = i * 4 + n
                low = jnp.where(v_of == i4, venergy[vband[i4 // nv, i4 % nv]], low)
            return low

        def conduction(i, high):
            return jnp.where(c_of == i, cenergy[cband[i // nc, i % nc]], high)

        low = lax.fori_loop(0, nblk * nv // 4, valence, jnp.zeros((8, LANE), jnp.float32))
        high = lax.fori_loop(0, nblk * nc, conduction, jnp.zeros((8, LANE), jnp.float32))
        delta = high - low
        scale = 1.0 / (8 * LANE) ** 0.5
        for w in range(NFREQ):
            value = -4.0 * delta / (delta * delta + (1.5 * w) ** 2) * scale
            for n in range(8):
                factors[w:w + 1, n * LANE:(n + 1) * LANE] = value[n:n + 1, :]
        pltpu.make_async_copy(factors, factor_out, factor_sem).start()

    def around(step):
        for d in (2, 1, 3):
            step(d, 0)

    def sum_x(g):
        def go(d, carry):
            to = lax.rem(x + d, 4)
            pltpu.make_async_remote_copy(
                total.at[own_rows(g, to)], landed.at[d - 1, quarter(g)], x_send.at[g], x_recv.at[g],
                device_id=at_x(to, core), device_id_type=MESH,
            ).start()
            return carry

        around(go)

    def y_copy(g):
        return pltpu.make_async_remote_copy(
            mid.at[quarter(g)], mid_landed.at[quarter(g)], y_send.at[g], y_recv.at[g],
            device_id=((1 - ylo) * 4 + x, col), device_id_type=MESH,
        )

    def sum_y(g):
        three = landed.at[:, quarter(g)]
        pltpu.make_async_copy(three, three, x_recv.at[g]).wait()
        value = total[own_rows(g, x), :]
        for d in range(3):
            value = value + landed[d, quarter(g), :]
        mid[quarter(g), :] = value
        y_copy(g).start()

    def spread_copy(g, k, zz, hh):
        block = spread.at[k, quarter(g)]
        return pltpu.make_async_remote_copy(
            block, block, spread_send, spread_recv.at[g, k], device_id=seat(zz, hh, core), device_id_type=MESH
        )

    def hand_rows(g):
        y_copy(g).wait_recv()
        value = (mid[quarter(g), :] + mid_landed[quarter(g), :]).astype(spread.dtype)

        @pl.when(source)
        def _():
            spread[mark, quarter(g), :] = value
            if g in FAR:
                spread_copy(g, mark, lax.rem(z + 2, 4), 1 - h).start()
                spread_copy(g, mark, lax.rem(z + 2, 4), h).start()
            for dz in (1, 3):
                spread_copy(g, mark, lax.rem(z + dz, 4), h).start()
            for dz in (1, 3):
                spread_copy(g, mark, lax.rem(z + dz, 4), 1 - h).start()
            spread_copy(g, mark, z, 1 - h).start()

        halves[0, quarter(g), :] = value[:, :m_half]
        halves[1, quarter(g), :] = value[:, m_half:]

    def spread_wait(g, k):
        block = spread.at[k, quarter(g)]
        pltpu.make_async_copy(block, block, spread_recv.at[g, k]).wait()

    def pass_z(g):
        @pl.when(place == 2)
        def _():
            for k in (2, 3):
                spread_wait(g, k)
                spread_copy(g, k, lax.rem(z + 1, 4), h).start()

        @pl.when(place == 3)
        def _():
            for k in (0, 1):
                spread_wait(g, k)
                spread_copy(g, k, lax.rem(z + 3, 4), h).start()

    def hand_cols(g):
        here = cols_out.at[pl.ds(pair_row(g, x, j, core), QUARTER[g])]

        def go_cols(d, carry):
            to = lax.rem(x + d, 4)
            for c in range(2):
                pltpu.make_async_remote_copy(
                    halves.at[c, quarter(g)], here, cols_send, cols_recv,
                    device_id=at_x(to, c), device_id_type=MESH,
                ).start()
            return carry

        around(go_cols)
        pltpu.make_async_remote_copy(
            halves.at[1 - core, quarter(g)], here, cols_send, cols_recv, device_id=twin, device_id_type=MESH
        ).start()
        pltpu.make_async_copy(halves.at[core, quarter(g)], here, local_sem.at[g]).start()

    def deal(g):
        for k in range(4):
            if g in FAR:
                pl.when(4 * ylo + k != j)(functools.partial(spread_wait, g, k))
            else:
                pl.when((4 * ylo + k != j) & (place != 3 - k // 2))(
                    functools.partial(spread_wait, g, k)
                )

        def there(to):
            return rows_out.at[pl.ds(pair_row(g, x, 4 * ylo + to, core), QUARTER[g])]

        def go(d, carry):
            to = lax.rem(x + d, 4)
            pltpu.make_async_remote_copy(
                spread.at[to, quarter(g)], there(to), rows_send, rows_recv.at[g],
                device_id=at_x(to, core), device_id_type=MESH,
            ).start()
            if g in BOTH:
                pltpu.make_async_remote_copy(
                    spread.at[to, quarter(g)], there(to), twin_send, twin_recv,
                    device_id=at_x(to, 1 - core), device_id_type=MESH,
                ).start()
            return carry

        around(go)
        kept = spread.at[x, quarter(g)]
        pltpu.make_async_copy(kept, there(x), local_sem.at[NG + g]).start()
        pltpu.make_async_remote_copy(
            kept, there(x), twin_send, twin_recv, device_id=twin, device_id_type=MESH
        ).start()

    def arrived(g):
        three = rows_out.at[pl.ds(0, 3 * QUARTER[g])]
        pltpu.make_async_copy(three, three, rows_recv.at[g]).wait()

    def pass_on(g):
        arrived(g)

        def go(d, carry):
            block = rows_out.at[pl.ds(pair_row(g, lax.rem(x + d, 4), row, core), QUARTER[g])]
            pltpu.make_async_remote_copy(
                block, block, twin_send, twin_recv, device_id=twin, device_id_type=MESH
            ).start()
            return carry

        around(go)

    local[0].wait()
    local[1].wait()
    send(0, "B", "up")
    send(0, "B", "down")
    send(0, "A", "across")
    eig_copy.start()
    send(0, "A", "up")
    send(0, "A", "down")
    send(0, "B", "across")
    pair_factors()
    local[2].wait()
    eig_copy.wait()
    multiply(0, 1, "B")
    multiply(0, 1, "A")
    sum_x(0)
    arrive(3, "B")
    send(3, "B1", "up")
    arrive(2, "B")
    send(2, "B2", "down")
    sum_y(0)
    send(3, "B", "across")
    send(2, "B", "across")
    arrive(1, "A")
    send(1, "A", "up")
    send(1, "A", "down")
    arrive(3, "A")
    send(3, "A1", "up")
    arrive(2, "A")
    send(2, "A2", "down")
    multiply(1, 4, "A")
    arrive(1, "B")
    multiply(1, 4, "B")
    sum_x(1)
    sum_x(2)
    arrive(6, "B1")
    arrive(6, "B2")
    multiply(6, 7, "B")
    sum_y(1)
    sum_y(2)
    send(6, "B1", "across")
    send(6, "B2", "across")
    arrive(5, "A")
    send(5, "A1a", "up")
    send(5, "A1b", "up")
    arrive(4, "A")
    send(4, "A2a", "down")
    send(4, "A2b", "down")
    hand_rows(0)
    hand_cols(0)
    arrive(5, "B")
    arrive(4, "B")
    multiply(4, 6, "B")
    hand_rows(1)
    hand_rows(2)
    hand_cols(1)
    hand_cols(2)
    multiply(4, 6, "A")
    sum_x(3)
    arrive(6, "A1")
    arrive(6, "A2")
    multiply(6, 7, "A")
    sum_x(4)
    arrive(7, "A1a")
    multiply(7, 8, "A1a")
    arrive(7, "A2a")
    multiply(7, 8, "A2a")
    arrive(7, "B1")
    arrive(7, "B2")
    multiply(7, 8, "B")
    arrive(7, "A1b")
    multiply(7, 8, "A1b")
    arrive(7, "A2b")
    multiply(7, 8, "A2b")
    sum_x(5)
    sum_y(3)
    sum_y(4)
    pass_z(0)
    pass_z(1)
    pass_z(2)
    hand_rows(3)
    sum_y(5)
    hand_rows(4)
    hand_cols(3)
    hand_cols(4)
    deal(0)
    deal(1)
    deal(2)
    hand_rows(5)
    hand_cols(5)
    deal(3)
    deal(4)
    pass_on(0)
    pass_on(1)
    pass_on(2)
    deal(5)
    pass_on(3)
    pass_on(4)
    arrived(5)

    pltpu.make_async_copy(factors, factor_out, factor_sem).wait()
    for c in copies.values():
        c.wait_send()
    for g in range(NG):
        three = landed.at[:, quarter(g)]
        pltpu.make_async_copy(three, three, x_send.at[g]).wait()
        y_copy(g).wait_send()
        for n, block in ((g, cols_out.at[pl.ds(0, QUARTER[g])]), (NG + g, rows_out.at[pl.ds(0, QUARTER[g])])):
            pltpu.make_async_copy(block, block, local_sem.at[n]).wait()

    def wait_rows(ref, count, s):
        block = ref.at[pl.ds(0, count)]
        pltpu.make_async_copy(block, block, s).wait()

    mine, far = sum(QUARTER), sum(QUARTER[g] for g in FAR)

    @pl.when(source)
    def _():
        wait_rows(rows_out, 5 * mine + 2 * far, spread_send)

    @pl.when(place >= 2)
    def _():
        wait_rows(rows_out, 2 * (mine - far), spread_send)

    wait_rows(cols_out, 7 * mine, cols_send)
    wait_rows(cols_out, 7 * mine, cols_recv)
    wait_rows(rows_out, 3 * mine, rows_send)
    wait_rows(rows_out, 4 * mine, twin_send)
    wait_rows(rows_out, 4 * mine, twin_recv)


def project(pairs_t, eig_t, *tables):
    nblk, pair_rows, depth = pairs_t.shape
    m_half = eig_t.shape[0]
    m_all = 2 * m_half
    bf16, f32 = jnp.bfloat16, jnp.float32
    dma = pltpu.SemaphoreType.DMA
    mine = sum(QUARTER)
    return pl.pallas_call(
        project_kernel,
        out_shape=(
            jax.ShapeDtypeStruct((1024, m_all), bf16),
            jax.ShapeDtypeStruct((1024, m_half), bf16),
            jax.ShapeDtypeStruct((NFREQ, 1024), f32),
        ),
        in_specs=[pl.BlockSpec(memory_space=pltpu.HBM)] * 6,
        out_specs=(pl.BlockSpec(memory_space=pl.ANY),) * 3,
        scratch_shapes=[
            pltpu.VMEM((512, depth), bf16),
            pltpu.VMEM((m_all, depth), bf16),
            pltpu.VMEM((512, m_all), f32),
            pltpu.VMEM((3, mine, m_all), f32),
            pltpu.VMEM((mine, m_all), f32),
            pltpu.VMEM((mine, m_all), f32),
            pltpu.VMEM((2, mine, m_half), bf16),
            pltpu.VMEM((4, mine, m_all), bf16),
            dma((20,)), dma((20,)), dma((3,)), dma, dma, dma((NG,)), dma((NG,)), dma((NG,)), dma((NG,)),
            dma, dma((NG, 4)), dma, dma, dma, dma((NG,)), dma, dma, dma((2 * NG,)),
            *(pltpu.SMEM(a.shape, a.dtype) for a in tables), pltpu.VMEM((NFREQ, 1024), f32), dma((4,)), dma,
        ],
        compiler_params=pltpu.CompilerParams(
            collective_id=0, has_side_effects=True, vmem_limit_bytes=48 * 2**20
        ),
        name="project",
    )(*(pltpu.with_memory_space_constraint(a, pltpu.HBM) for a in (pairs_t, eig_t, *tables)))


def chi_kernel(factor_ref, rows_ref, cols_ref, out_ref, cols_t, scaled):
    @pl.when(pl.program_id(0) == 0)
    def _():
        cols_t[...] = cols_ref[...].T

    s_cols = cols_t.shape[0]
    for w in range(STEP):
        scaled[w * s_cols:(w + 1) * s_cols] = (
            cols_t[...].astype(jnp.float32) * factor_ref[pl.ds(pl.program_id(0) * STEP + w, 1), :]
        ).astype(scaled.dtype)
    value = jnp.dot(scaled[...], rows_ref[...], preferred_element_type=jnp.float32)
    out_ref[...] = value.reshape(out_ref.shape)


def polarizability(factor, rows, cols):
    n, s_rows = rows.shape
    s_cols = cols.shape[1]
    return pl.pallas_call(
        chi_kernel,
        grid=(NFREQ // STEP,),
        out_shape=jax.ShapeDtypeStruct((NFREQ, s_cols, s_rows), jnp.float32),
        in_specs=[pl.BlockSpec(memory_space=pltpu.VMEM)] * 3,
        out_specs=pl.BlockSpec((STEP, s_cols, s_rows), lambda w: (w, 0, 0)),
        scratch_shapes=[pltpu.VMEM((s_cols, n), jnp.bfloat16), pltpu.VMEM((STEP * s_cols, n), jnp.bfloat16)],
        compiler_params=pltpu.CompilerParams(vmem_limit_bytes=32 * 2**20),
        name="chi",
    )(factor, rows, cols)


def local(pair_products, eigvecs, valence_band, cond_band, valence_energy, cond_energy):
    rows, cols, factor = project(
        pair_products.transpose(0, 2, 1), eigvecs.T, valence_band, cond_band, valence_energy, cond_energy
    )
    return polarizability(factor, rows, cols).transpose(0, 2, 1)


def solution(mesh):
    return jax.shard_map(
        local,
        mesh=mesh,
        in_specs=(P(None, "row", "col"), P("row", "col"), P(), P(), P(), P()),
        out_specs=P(None, "row", "col"),
        check_vma=False,
    )
```

```python
import functools

import jax
import jax.numpy as jnp
from jax import lax
from jax.experimental import pallas as pl
from jax.experimental.pallas import tpu as pltpu
from jax.sharding import PartitionSpec as P

NFREQ = 12
STEP = 3
MESH = pl.DeviceIdType.MESH
LANE = 128
TA1, TA2, TB1, TB2 = 14, 14, 9, 8
GROUP = (0, 64, 128, 256, 384, 448)
QUARTER = (16, 16, 32, 32, 16, 16)
NG = len(GROUP)
FAR = (3, 4, 5)
BOTH = (5,)


def project_kernel(p_hbm, e_hbm, vband_hbm, cband_hbm, venergy_hbm, cenergy_hbm, rows_out, cols_out, factor_out,
                   pairs, eig, total, landed, mid, mid_landed, halves, spread,
                   gather_send, gather_recv, copy_sem, eig_send, eig_recv, x_send, x_recv, y_send, y_recv,
                   spread_send, spread_recv, cols_send, cols_recv, rows_send, rows_recv, twin_send, twin_recv, local_sem,
                   vband, cband, venergy, cenergy, factors, table_sem, factor_sem):
    row, col = lax.axis_index("row"), lax.axis_index("col")
    core = lax.rem(col, 2)
    j = col // 2
    z, h = j // 2, lax.rem(j, 2)
    ylo, x = row // 4, lax.rem(row, 4)
    m_half = e_hbm.shape[0]
    source, mark = z // 2 == ylo, lax.rem(j, 4)
    place = lax.rem(z + 4 - 2 * ylo, 4)

    def seat(zz, hh, cc):
        return (row, zz * 4 + hh * 2 + cc)

    up = seat(lax.rem(z + 1, 4), h, core)
    down = seat(lax.rem(z + 3, 4), h, core)
    across = seat(z, 1 - h, core)
    twin = (row, col + 1 - 2 * core)

    block_rows = p_hbm.shape[1]
    local = [
        pltpu.make_async_copy(p_hbm.at[b], pairs.at[pl.ds(b * block_rows, block_rows)], copy_sem.at[b])
        for b in range(2)
    ]
    mine = pl.ds(pl.multiple_of(core * m_half, 16), m_half)
    local.append(pltpu.make_async_copy(e_hbm, eig.at[mine], copy_sem.at[2]))
    for c in local:
        c.start()

    tables = [
        pltpu.make_async_copy(src, dst, table_sem.at[n])
        for n, (src, dst) in enumerate(
            ((vband_hbm, vband), (cband_hbm, cband), (venergy_hbm, venergy), (cenergy_hbm, cenergy))
        )
    ]
    for c in tables:
        c.start()

    barrier = pltpu.get_barrier_semaphore()

    def greet_rows(d, carry):
        other = ylo * 4 + lax.rem(x + d, 4)
        for c in range(2):
            pl.semaphore_signal(barrier, inc=1, device_id=(other, j * 2 + c), device_id_type=MESH)
        return carry

    def greet_cols(d, carry):
        other = lax.rem(j + d, 8)
        pl.semaphore_signal(barrier, inc=1, device_id=(row, other * 2 + core), device_id_type=MESH)
        return carry

    lax.fori_loop(1, 4, greet_rows, 0)
    lax.fori_loop(1, 8, greet_cols, 0)
    for other in (twin, ((1 - ylo) * 4 + x, col)):
        pl.semaphore_signal(barrier, inc=1, device_id=other, device_id_type=MESH)
    pl.semaphore_wait(barrier, 15)

    eig_copy = pltpu.make_async_remote_copy(
        e_hbm, eig.at[mine], eig_send, eig_recv, device_id=twin, device_id_type=MESH
    )

    a0, a1, a2 = 0, TA1 * LANE, (TA1 + TA2) * LANE
    b1, b2 = a2 + TB1 * LANE, a2 + (TB1 + TB2) * LANE
    piece = {"A": (a0, a2), "A1": (a0, a1), "A2": (a1, a2), "B": (a2, b2), "B1": (a2, b1), "B2": (b1, b2)}
    for name in ("A1", "A2"):
        lo, hi = piece[name]
        cut = lo + (hi - lo) // (2 * LANE) * LANE
        piece[name + "a"], piece[name + "b"] = (lo, cut), (cut, hi)

    slot_of = {(0, 0): 0, (0, 1): 1, (1, 0): 2, (3, 0): 3, (1, 1): 4, (3, 1): 5, (2, 0): 6, (2, 1): 7}
    place_of = {s: k for k, s in slot_of.items()}
    copies = {}
    begun = set()

    def region(slot, name):
        lo, hi = piece[name]
        return pairs.at[pl.ds(64 * slot, 64), pl.ds(lo, hi - lo)]

    def send(slot, name, way):
        dz, dh = place_of[slot]
        target, there = {
            "up": (up, ((dz + 3) % 4, dh)),
            "down": (down, ((dz + 1) % 4, dh)),
            "across": (across, (dz, 1 - dh)),
        }[way]
        there = slot_of[there]
        n = len(copies)
        c = pltpu.make_async_remote_copy(
            region(slot, name), region(there, name), gather_send.at[n], gather_recv.at[n],
            device_id=target, device_id_type=MESH,
        )
        copies[(there, name)] = c
        c.start()

    def arrive(slot, name):
        copies[(slot, name)].wait_recv()

    def multiply(first, last, name):
        lo, hi = piece[name]
        rows = pl.ds(64 * first, 64 * (last - first))
        value = lax.dot_general(
            pairs[rows, lo:hi], eig[:, lo:hi], (((1,), (1,)), ((), ())), preferred_element_type=jnp.float32
        )
        if first in begun:
            total[rows, :] += value
        else:
            total[rows, :] = value
        begun.update(range(first, last))

    def quarter(g):
        return pl.ds(sum(QUARTER[:g]), QUARTER[g])

    def pair_row(g, owner, jj, cc):
        if QUARTER[g] == 32:
            dz, dh, at = 1 + 2 * (owner // 2), g - 2, 32 * lax.rem(owner, 2)
        else:
            dz, dh, at = 2 * (g // 4), g % 2 if g < 2 else g - 4, 16 * owner
        zz = lax.rem(jj // 2 + dz, 4)
        hh = lax.rem(lax.rem(jj, 2) + dh, 2)
        return pl.multiple_of(cc * 512 + (zz * 2 + hh) * 64 + at, 16)

    def at_x(xx, cc):
        return (ylo * 4 + xx, j * 2 + cc)

    def own_rows(g, xx):
        return pl.ds(pl.multiple_of(GROUP[g] + xx * QUARTER[g], 16), QUARTER[g])

    def pair_factors():
        for c in tables:
            c.wait()
        nblk, nv = vband.shape
        nc = cband.shape[1]
        part_of = lax.broadcasted_iota(jnp.int32, (8, LANE), 0)
        lane = lax.broadcasted_iota(jnp.int32, (8, LANE), 1)
        blk = (lane // 32) % 2
        v_of = blk * nv + ((part_of % 4) * 2 + lane // 64) * 8 + (part_of // 4) * 4 + (lane % 32) // 8
        c_of = blk * nc + lane % 8

        def valence(i, low):
            for n in range(4):
                i4 = i * 4 + n
                low = jnp.where(v_of == i4, venergy[vband[i4 // nv, i4 % nv]], low)
            return low

        def conduction(i, high):
            return jnp.where(c_of == i, cenergy[cband[i // nc, i % nc]], high)

        low = lax.fori_loop(0, nblk * nv // 4, valence, jnp.zeros((8, LANE), jnp.float32))
        high = lax.fori_loop(0, nblk * nc, conduction, jnp.zeros((8, LANE), jnp.float32))
        delta = high - low
        scale = 1.0 / (8 * LANE) ** 0.5
        for w in range(NFREQ):
            value = -4.0 * delta / (delta * delta + (1.5 * w) ** 2) * scale
            for n in range(8):
                factors[w:w + 1, n * LANE:(n + 1) * LANE] = value[n:n + 1, :]
        pltpu.make_async_copy(factors, factor_out, factor_sem).start()

    def around(step):
        for d in (2, 1, 3):
            step(d, 0)

    def sum_x(g):
        def go(d, carry):
            to = lax.rem(x + d, 4)
            pltpu.make_async_remote_copy(
                total.at[own_rows(g, to)], landed.at[d - 1, quarter(g)], x_send.at[g], x_recv.at[g],
                device_id=at_x(to, core), device_id_type=MESH,
            ).start()
            return carry

        around(go)

    def y_copy(g):
        return pltpu.make_async_remote_copy(
            mid.at[quarter(g)], mid_landed.at[quarter(g)], y_send.at[g], y_recv.at[g],
            device_id=((1 - ylo) * 4 + x, col), device_id_type=MESH,
        )

    def sum_y(g):
        three = landed.at[:, quarter(g)]
        pltpu.make_async_copy(three, three, x_recv.at[g]).wait()
        value = total[own_rows(g, x), :]
        for d in range(3):
            value = value + landed[d, quarter(g), :]
        mid[quarter(g), :] = value
        y_copy(g).start()

    def spread_copy(g, k, zz, hh):
        block = spread.at[k, quarter(g)]
        return pltpu.make_async_remote_copy(
            block, block, spread_send, spread_recv.at[g, k], device_id=seat(zz, hh, core), device_id_type=MESH
        )

    def hand_rows(g):
        y_copy(g).wait_recv()
        value = (mid[quarter(g), :] + mid_landed[quarter(g), :]).astype(spread.dtype)

        @pl.when(source)
        def _():
            spread[mark, quarter(g), :] = value
            if g in FAR:
                spread_copy(g, mark, lax.rem(z + 2, 4), 1 - h).start()
                spread_copy(g, mark, lax.rem(z + 2, 4), h).start()
            for dz in (1, 3):
                spread_copy(g, mark, lax.rem(z + dz, 4), h).start()
            for dz in (1, 3):
                spread_copy(g, mark, lax.rem(z + dz, 4), 1 - h).start()
            spread_copy(g, mark, z, 1 - h).start()

        halves[0, quarter(g), :] = value[:, :m_half]
        halves[1, quarter(g), :] = value[:, m_half:]

    def spread_wait(g, k):
        block = spread.at[k, quarter(g)]
        pltpu.make_async_copy(block, block, spread_recv.at[g, k]).wait()

    def pass_z(g):
        @pl.when(place == 2)
        def _():
            for k in (2, 3):
                spread_wait(g, k)
                spread_copy(g, k, lax.rem(z + 1, 4), h).start()

        @pl.when(place == 3)
        def _():
            for k in (0, 1):
                spread_wait(g, k)
                spread_copy(g, k, lax.rem(z + 3, 4), h).start()

    def hand_cols(g):
        here = cols_out.at[pl.ds(pair_row(g, x, j, core), QUARTER[g])]

        def go_cols(d, carry):
            to = lax.rem(x + d, 4)
            for c in range(2):
                pltpu.make_async_remote_copy(
                    halves.at[c, quarter(g)], here, cols_send, cols_recv,
                    device_id=at_x(to, c), device_id_type=MESH,
                ).start()
            return carry

        around(go_cols)
        pltpu.make_async_remote_copy(
            halves.at[1 - core, quarter(g)], here, cols_send, cols_recv, device_id=twin, device_id_type=MESH
        ).start()
        pltpu.make_async_copy(halves.at[core, quarter(g)], here, local_sem.at[g]).start()

    def deal(g):
        for k in range(4):
            if g in FAR:
                pl.when(4 * ylo + k != j)(functools.partial(spread_wait, g, k))
            else:
                pl.when((4 * ylo + k != j) & (place != 3 - k // 2))(
                    functools.partial(spread_wait, g, k)
                )

        def there(to):
            return rows_out.at[pl.ds(pair_row(g, x, 4 * ylo + to, core), QUARTER[g])]

        def go(d, carry):
            to = lax.rem(x + d, 4)
            pltpu.make_async_remote_copy(
                spread.at[to, quarter(g)], there(to), rows_send, rows_recv.at[g],
                device_id=at_x(to, core), device_id_type=MESH,
            ).start()
            if g in BOTH:
                pltpu.make_async_remote_copy(
                    spread.at[to, quarter(g)], there(to), twin_send, twin_recv,
                    device_id=at_x(to, 1 - core), device_id_type=MESH,
                ).start()
            return carry

        around(go)
        kept = spread.at[x, quarter(g)]
        pltpu.make_async_copy(kept, there(x), local_sem.at[NG + g]).start()
        pltpu.make_async_remote_copy(
            kept, there(x), twin_send, twin_recv, device_id=twin, device_id_type=MESH
        ).start()

    def arrived(g):
        three = rows_out.at[pl.ds(0, 3 * QUARTER[g])]
        pltpu.make_async_copy(three, three, rows_recv.at[g]).wait()

    def pass_on(g):
        arrived(g)

        def go(d, carry):
            block = rows_out.at[pl.ds(pair_row(g, lax.rem(x + d, 4), row, core), QUARTER[g])]
            pltpu.make_async_remote_copy(
                block, block, twin_send, twin_recv, device_id=twin, device_id_type=MESH
            ).start()
            return carry

        around(go)

    local[0].wait()
    local[1].wait()
    send(0, "B", "up")
    send(0, "B", "down")
    send(0, "A", "across")
    eig_copy.start()
    send(0, "A", "up")
    send(0, "A", "down")
    send(0, "B", "across")
    pair_factors()
    local[2].wait()
    eig_copy.wait()
    multiply(0, 1, "B")
    multiply(0, 1, "A")
    sum_x(0)
    arrive(3, "B")
    send(3, "B1", "up")
    arrive(2, "B")
    send(2, "B2", "down")
    sum_y(0)
    send(3, "B", "across")
    send(2, "B", "across")
    arrive(1, "A")
    send(1, "A", "up")
    send(1, "A", "down")
    arrive(3, "A")
    send(3, "A1", "up")
    arrive(2, "A")
    send(2, "A2", "down")
    multiply(1, 4, "A")
    arrive(1, "B")
    multiply(1, 4, "B")
    sum_x(1)
    sum_x(2)
    arrive(6, "B1")
    arrive(6, "B2")
    multiply(6, 7, "B")
    sum_y(1)
    sum_y(2)
    send(6, "B1", "across")
    send(6, "B2", "across")
    arrive(5, "A")
    send(5, "A1a", "up")
    send(5, "A1b", "up")
    arrive(4, "A")
    send(4, "A2a", "down")
    send(4, "A2b", "down")
    hand_rows(0)
    hand_cols(0)
    arrive(5, "B")
    arrive(4, "B")
    multiply(4, 6, "B")
    hand_rows(1)
    hand_rows(2)
    hand_cols(1)
    hand_cols(2)
    multiply(4, 6, "A")
    sum_x(3)
    arrive(6, "A1")
    arrive(6, "A2")
    multiply(6, 7, "A")
    sum_x(4)
    arrive(7, "A1a")
    multiply(7, 8, "A1a")
    arrive(7, "A2a")
    multiply(7, 8, "A2a")
    arrive(7, "B1")
    arrive(7, "B2")
    multiply(7, 8, "B")
    arrive(7, "A1b")
    multiply(7, 8, "A1b")
    arrive(7, "A2b")
    multiply(7, 8, "A2b")
    sum_x(5)
    sum_y(3)
    sum_y(4)
    pass_z(0)
    pass_z(1)
    pass_z(2)
    hand_rows(3)
    hand_cols(3)
    sum_y(5)
    hand_rows(4)
    hand_cols(4)
    deal(0)
    deal(1)
    deal(2)
    hand_rows(5)
    hand_cols(5)
    deal(3)
    pass_on(0)
    pass_on(1)
    deal(4)
    pass_on(2)
    deal(5)
    pass_on(3)
    pass_on(4)
    arrived(5)

    pltpu.make_async_copy(factors, factor_out, factor_sem).wait()
    for c in copies.values():
        c.wait_send()
    for g in range(NG):
        three = landed.at[:, quarter(g)]
        pltpu.make_async_copy(three, three, x_send.at[g]).wait()
        y_copy(g).wait_send()
        for n, block in ((g, cols_out.at[pl.ds(0, QUARTER[g])]), (NG + g, rows_out.at[pl.ds(0, QUARTER[g])])):
            pltpu.make_async_copy(block, block, local_sem.at[n]).wait()

    def wait_rows(ref, count, s):
        block = ref.at[pl.ds(0, count)]
        pltpu.make_async_copy(block, block, s).wait()

    mine, far = sum(QUARTER), sum(QUARTER[g] for g in FAR)

    @pl.when(source)
    def _():
        wait_rows(rows_out, 5 * mine + 2 * far, spread_send)

    @pl.when(place >= 2)
    def _():
        wait_rows(rows_out, 2 * (mine - far), spread_send)

    wait_rows(cols_out, 7 * mine, cols_send)
    wait_rows(cols_out, 7 * mine, cols_recv)
    wait_rows(rows_out, 3 * mine, rows_send)
    wait_rows(rows_out, 4 * mine, twin_send)
    wait_rows(rows_out, 4 * mine, twin_recv)


def project(pairs_t, eig_t, *tables):
    nblk, pair_rows, depth = pairs_t.shape
    m_half = eig_t.shape[0]
    m_all = 2 * m_half
    bf16, f32 = jnp.bfloat16, jnp.float32
    dma = pltpu.SemaphoreType.DMA
    mine = sum(QUARTER)
    return pl.pallas_call(
        project_kernel,
        out_shape=(
            jax.ShapeDtypeStruct((1024, m_all), bf16),
            jax.ShapeDtypeStruct((1024, m_half), bf16),
            jax.ShapeDtypeStruct((NFREQ, 1024), f32),
        ),
        in_specs=[pl.BlockSpec(memory_space=pltpu.HBM)] * 6,
        out_specs=(pl.BlockSpec(memory_space=pl.ANY),) * 3,
        scratch_shapes=[
            pltpu.VMEM((512, depth), bf16),
            pltpu.VMEM((m_all, depth), bf16),
            pltpu.VMEM((512, m_all), f32),
            pltpu.VMEM((3, mine, m_all), f32),
            pltpu.VMEM((mine, m_all), f32),
            pltpu.VMEM((mine, m_all), f32),
            pltpu.VMEM((2, mine, m_half), bf16),
            pltpu.VMEM((4, mine, m_all), bf16),
            dma((20,)), dma((20,)), dma((3,)), dma, dma, dma((NG,)), dma((NG,)), dma((NG,)), dma((NG,)),
            dma, dma((NG, 4)), dma, dma, dma, dma((NG,)), dma, dma, dma((2 * NG,)),
            *(pltpu.SMEM(a.shape, a.dtype) for a in tables), pltpu.VMEM((NFREQ, 1024), f32), dma((4,)), dma,
        ],
        compiler_params=pltpu.CompilerParams(
            collective_id=0, has_side_effects=True, vmem_limit_bytes=48 * 2**20
        ),
        name="project",
    )(*(pltpu.with_memory_space_constraint(a, pltpu.HBM) for a in (pairs_t, eig_t, *tables)))


def chi_kernel(factor_ref, rows_ref, cols_ref, out_ref, cols_t, scaled):
    @pl.when(pl.program_id(0) == 0)
    def _():
        cols_t[...] = cols_ref[...].T

    s_cols = cols_t.shape[0]
    for w in range(STEP):
        scaled[w * s_cols:(w + 1) * s_cols] = (
            cols_t[...].astype(jnp.float32) * factor_ref[pl.ds(pl.program_id(0) * STEP + w, 1), :]
        ).astype(scaled.dtype)
    value = jnp.dot(scaled[...], rows_ref[...], preferred_element_type=jnp.float32)
    out_ref[...] = value.reshape(out_ref.shape)


def polarizability(factor, rows, cols):
    n, s_rows = rows.shape
    s_cols = cols.shape[1]
    return pl.pallas_call(
        chi_kernel,
        grid=(NFREQ // STEP,),
        out_shape=jax.ShapeDtypeStruct((NFREQ, s_cols, s_rows), jnp.float32),
        in_specs=[pl.BlockSpec(memory_space=pltpu.VMEM)] * 3,
        out_specs=pl.BlockSpec((STEP, s_cols, s_rows), lambda w: (w, 0, 0)),
        scratch_shapes=[pltpu.VMEM((s_cols, n), jnp.bfloat16), pltpu.VMEM((STEP * s_cols, n), jnp.bfloat16)],
        compiler_params=pltpu.CompilerParams(vmem_limit_bytes=32 * 2**20),
        name="chi",
    )(factor, rows, cols)


def local(pair_products, eigvecs, valence_band, cond_band, valence_energy, cond_energy):
    rows, cols, factor = project(
        pair_products.transpose(0, 2, 1), eigvecs.T, valence_band, cond_band, valence_energy, cond_energy
    )
    return polarizability(factor, rows, cols).transpose(0, 2, 1)


def solution(mesh):
    return jax.shard_map(
        local,
        mesh=mesh,
        in_specs=(P(None, "row", "col"), P("row", "col"), P(), P(), P(), P()),
        out_specs=P(None, "row", "col"),
        check_vma=False,
    )
```
